32 devices in a mesh: azim: 4 (over z), rad: 4 (over x, core), axial: 2 (over y).
Axes of the slice: x: 2, y: 2, z: 4, core: 2. Of those that a mesh axis runs over, the one named last changes fastest.
Arguments:
- residual: float32 [5, 128, 64, 256], P(None, 'azim', 'rad', 'axial'), may hold values from -12 to 12
- left_vec: float32 [5, 5], replicated, may hold values from -2.5 to 2.5
- dissip: float32 [5], replicated, may hold values from 0.2 to 0.5
- azim_coef: float32 [4, 5, 128], replicated, may hold values from 0 to 1, as said below
- radial_coef: float32 [2, 5, 64], replicated, may hold values from 0 to 3328
Outputs:
- update: float32 [5, 128, 64, 256], P(None, 'azim', 'rad', 'axial')
The draws below stay inside these ranges and needn't reach their ends.
Inputs may be any that keep to these rules, and one draw needn't show every extreme that they name: `azim_coef`: at every position a and b are positive with a + b < 1, and so are c and e with c + e < 1.
All inputs are finite; a program needn't handle non-finite values.
Results may differ from the reference program's by a relative error of at most 0.0003.
Values sent between devices are 32-bit elements; how exact they have to be, the bound alone decides.
No kernel may reach another device: no remote copies, remote signals or barrier semaphores. Data moves between devices by JAX's collectives and lax.ppermute only.
A program may use at most 64 MiB of HBM per device.

```python
import math
import jax
import jax.numpy as jnp
from jax import lax

FIELD_COUNT = 5
CA = 32
CR = 16
AZIMUTH_CELLS = 128
NR = 64
NX = 256


def field_rates(key, fast_count):
    random_subkey_list = jax.random.split(key, 8)
    ranking = jax.random.permutation(random_subkey_list[0], FIELD_COUNT)
    fast_flag = (ranking < fast_count).astype(jnp.float32)[:, None]
    blocks = AZIMUTH_CELLS // CA
    slow_tau = AZIMUTH_CELLS * jnp.exp(jax.random.uniform(random_subkey_list[1], (FIELD_COUNT, 1), jnp.float32, math.log(2.0), math.log(4.0)))
    fast_tau = jnp.exp(jax.random.uniform(random_subkey_list[2], (FIELD_COUNT, 1), jnp.float32, math.log(8.0), math.log(16.0)))
    field_tau = fast_flag * fast_tau + (1.0 - fast_flag) * slow_tau
    block_factor = jnp.exp(jax.random.uniform(random_subkey_list[3], (FIELD_COUNT, blocks, 1), jnp.float32, math.log(0.7), math.log(1.4)))
    block_factor = jnp.broadcast_to(block_factor, (FIELD_COUNT, blocks, CA)).reshape(FIELD_COUNT, AZIMUTH_CELLS)
    cell_factor = jnp.exp(jax.random.uniform(random_subkey_list[4], (FIELD_COUNT, AZIMUTH_CELLS), jnp.float32, math.log(0.7), math.log(1.4)))
    tau_line = field_tau * block_factor * cell_factor
    retained = 1.0 - 1.0 / tau_line
    share_two = jax.random.uniform(random_subkey_list[5], (FIELD_COUNT, AZIMUTH_CELLS), jnp.float32, 0.1, 0.3)
    pulse_location = jax.random.randint(random_subkey_list[6], (FIELD_COUNT, 2), 0, AZIMUTH_CELLS)
    pulse_decay = jax.random.uniform(random_subkey_list[7], (FIELD_COUNT, 2), jnp.float32, 0.6, 0.8)
    cell_locations = jnp.arange(AZIMUTH_CELLS)
    impact_count = cell_locations[None, None, :] == pulse_location[:, :, None]
    damping_factor = jnp.prod(jnp.where(impact_count, pulse_decay[:, :, None], 1.0), axis=1)
    return (retained * (1.0 - share_two) * damping_factor, retained * share_two * damping_factor)


def draw_azim_coef(key, part):
    fast_count = jax.random.randint(jax.random.fold_in(key, 7), (), 1, 4)
    first, second = field_rates(jax.random.fold_in(key, 1), fast_count)
    third, fourth = field_rates(jax.random.fold_in(key, 2), fast_count)
    return jnp.stack([first, second, third, fourth])


def draw_radial_coef(key, part):
    random_subkey_list = jax.random.split(key, 6)
    fast_count = jax.random.randint(random_subkey_list[0], (), 1, 3)
    ranking = jax.random.permutation(random_subkey_list[1], FIELD_COUNT)
    fast_flag = (ranking < fast_count).astype(jnp.float32)[:, None]
    slow_len = CR * jnp.exp(jax.random.uniform(random_subkey_list[2], (FIELD_COUNT, 1), jnp.float32, math.log(1.5), math.log(2.5)))
    fast_len = jnp.exp(jax.random.uniform(random_subkey_list[3], (FIELD_COUNT, 1), jnp.float32, math.log(0.5), math.log(2.0)))
    length = fast_flag * fast_len + (1.0 - fast_flag) * slow_len
    strength = length * length
    lower = strength * jnp.exp(jax.random.uniform(random_subkey_list[4], (FIELD_COUNT, NR), jnp.float32, math.log(0.5), math.log(2.0)))
    upper = strength * jnp.exp(jax.random.uniform(random_subkey_list[5], (FIELD_COUNT, NR), jnp.float32, math.log(0.5), math.log(2.0)))
    return jnp.stack([lower, upper])


def draw_residual(key, part):
    random_subkey_list = jax.random.split(key, 1)
    noise = jax.random.normal(random_subkey_list[0], (FIELD_COUNT, AZIMUTH_CELLS, NR, NX), jnp.float32)
    values = noise
    return jnp.clip(values, -12.0, 12.0)


def centred(rng, extent, deviation, most, held_as=jnp.bfloat16):
    result = deviation * jax.random.normal(rng, extent, jnp.float32)
    return jnp.clip(result, min=-most, max=most).astype(held_as)


def setup_inputs(seed: int = 0) -> dict:
    splits = jax.random.split(jax.random.key(seed), 6)
    residual = draw_residual(jax.random.fold_in(splits[5], 71), 0)
    left_vec = centred(splits[1], (FIELD_COUNT, FIELD_COUNT), FIELD_COUNT ** -0.5, 2.5, jnp.float32)
    dissip = jnp.clip(jnp.exp(jax.random.uniform(splits[2], (FIELD_COUNT,), jnp.float32, math.log(0.2), math.log(0.5))), 0.2, 0.5)
    azim_coef = draw_azim_coef(jax.random.fold_in(splits[5], 71), 0)
    radial_coef = draw_radial_coef(jax.random.fold_in(splits[5], 71), 0)
    return {"residual": residual, "left_vec": left_vec, "dissip": dissip, "azim_coef": azim_coef, "radial_coef": radial_coef}


def azim_solve(source, first_coef, second_coef, direction):
    identity = jnp.eye(AZIMUTH_CELLS, dtype=jnp.float32)
    one_step = jnp.roll(identity, -direction, axis=1)
    two_step = jnp.roll(identity, -2 * direction, axis=1)
    matrix = identity[None] - first_coef[:, :, None] * one_step[None] - second_coef[:, :, None] * two_step[None]
    weights = jnp.sqrt(1.0 - (first_coef + second_coef) ** 2)
    right_side = (source * weights[:, :, None, None]).reshape(FIELD_COUNT, AZIMUTH_CELLS, NR * NX)
    solved = jnp.linalg.solve(matrix, right_side)
    return solved.reshape(FIELD_COUNT, AZIMUTH_CELLS, NR, NX)

def reference(residual, left_vec, dissip, azim_coef, radial_coef):
    characteristic = jnp.einsum('gf,farx->garx', left_vec, residual, precision=lax.Precision.HIGHEST)
    padded = jnp.pad(characteristic, ((0, 0), (0, 0), (0, 0), (1, 1)))
    source = characteristic + dissip[:, None, None, None] * (padded[..., 2:] + padded[..., :-2] - 2.0 * characteristic)
    lower_out = azim_solve(source, azim_coef[0], azim_coef[1], 1)
    upper_out = azim_solve(lower_out, azim_coef[2], azim_coef[3], -1)
    lower_rad = radial_coef[0]
    upper_rad = radial_coef[1]
    diagonal = 1.0 + lower_rad + upper_rad
    row_scale = diagonal ** 0.25
    below_diag = jnp.concatenate([jnp.zeros_like(lower_rad[:, :1]), -lower_rad[:, 1:]], axis=1)
    above_diag = jnp.concatenate([-upper_rad[:, :-1], jnp.zeros_like(upper_rad[:, :1])], axis=1)
    batch_shape = (FIELD_COUNT, AZIMUTH_CELLS, NR)
    return lax.linalg.tridiagonal_solve(jnp.broadcast_to(below_diag[:, None, :], batch_shape), jnp.broadcast_to(diagonal[:, None, :], batch_shape), jnp.broadcast_to(above_diag[:, None, :], batch_shape), upper_out * row_scale[:, None, :, None])
```

```python
import functools

import jax
import jax.numpy as jnp
from jax import lax
from jax.experimental import pallas as pl
from jax.experimental.pallas import tpu as pltpu
from jax.sharding import PartitionSpec as P

f32 = jnp.float32
VMEM = pl.BlockSpec(memory_space=pltpu.VMEM)
SMEM = pl.BlockSpec(memory_space=pltpu.SMEM)
params = pltpu.CompilerParams(vmem_limit_bytes=32 * 1024 * 1024)


def call(body, outs, n_smem, n_vmem, scratch=(), cost=None):
    return pl.pallas_call(
        body,
        out_shape=[jax.ShapeDtypeStruct(shape, f32) for shape in outs],
        in_specs=[SMEM] * n_smem + [VMEM] * n_vmem,
        out_specs=[VMEM] * len(outs),
        scratch_shapes=[pltpu.VMEM(shape, f32) for shape in scratch],
        compiler_params=params,
        cost_estimate=cost,
    )


def lanes_of(shape):
    return lax.broadcasted_iota(jnp.int32, shape, len(shape) - 1)


def edge_kernel(res_ref, edge_ref):
    fields, cells, rows, width = res_ref.shape
    source = jnp.where(lax.axis_index("axial") == 0, width - 1, 0)
    lane = lanes_of((rows, width))

    def step(j, packed):
        return tuple(
            jnp.where(lane == j, pltpu.roll(res_ref[f, j], (j - source + width) % width, 1), packed[f])
            for f in range(fields)
        )

    edge_ref[...] = jnp.zeros(edge_ref.shape, f32)
    packed = lax.fori_loop(0, cells, step, tuple(edge_ref[f] for f in range(fields)), unroll=4)
    for f in range(fields):
        edge_ref[f] = packed[f]


def first_kernel(coef_ref, vec_ref, dis_ref, res_ref, halo_ref, src_ref, state_ref, z_ref):
    fields, cells, rows, width = res_ref.shape
    tile = (rows, width)
    lane = lanes_of(tile)
    target = jnp.where(lax.axis_index("axial") == 0, width - 1, 0)
    vec = [[vec_ref[g * fields + f] for f in range(fields)] for g in range(fields)]
    dis = [dis_ref[g] for g in range(fields)]

    def mix(values):
        return [sum(vec[g][f] * values[f] for f in range(fields)) for g in range(fields)]

    halo = [dis[g] * h for g, h in enumerate(mix([halo_ref[f] for f in range(fields)]))]

    def coef(kind, f, j):
        return coef_ref[(kind * fields + f) * cells + j]

    def down(j, carry):
        chars = mix([res_ref[f, j] for f in range(fields)])
        out = []
        for f in range(fields):
            one, two = carry[f]
            c = chars[f]
            beside = jnp.where(lane == 0, 0.0, pltpu.roll(c, 1, 1)) + jnp.where(
                lane == width - 1, 0.0, pltpu.roll(c, width - 1, 1)
            )
            src = (1.0 - 2.0 * dis[f]) * c + dis[f] * beside
            src = src + jnp.where(
                lane == target, pltpu.roll(halo[f], (target - j + width) % width, 1), 0.0
            )
            src_ref[f, j] = src
            z = coef(2, f, j) * src + coef(1, f, j) * two + coef(0, f, j) * one
            z_ref[f, j] = z
            out.append((z, one))
        return tuple(out)

    state_ref[...] = jnp.zeros(state_ref.shape, f32)
    start = tuple((state_ref[f, 0], state_ref[f, 1]) for f in range(fields))
    carry = lax.fori_loop(0, cells, down, start, unroll=2)
    for f in range(fields):
        state_ref[f, 0], state_ref[f, 1] = carry[f]

    def up(i, carry):
        j = cells - 1 - i
        out = []
        for f in range(fields):
            one, two = carry[f]
            v = coef(5, f, j) * z_ref[f, j] + coef(4, f, j) * two + coef(3, f, j) * one
            out.append((v, one))
        return tuple(out)

    start = tuple((state_ref[f, 2], state_ref[f, 3]) for f in range(fields))
    carry = lax.fori_loop(0, cells, up, start, unroll=4)
    for f in range(fields):
        state_ref[f, 2], state_ref[f, 3] = carry[f]


def second_kernel(coef_ref, enter_ref, rad_ref, *refs):
    states, (src_ref, line_ref, end_ref, z_ref) = refs[:-4], refs[-4:]
    fields, cells, rows, width = src_ref.shape
    tile = (rows, width)
    slots = 4 * len(states)

    def coef(kind, f, j):
        return coef_ref[(kind * fields + f) * cells + j]

    entry = []
    for f in range(fields):
        sums = []
        for m in range(4):
            total = jnp.zeros(tile, f32)
            for k in range(slots):
                total = total + enter_ref[(m * slots + k) * fields + f] * states[k // 4][f, k % 4]
            sums.append(total)
        entry.append(sums)

    def down(j, carry):
        out = []
        for f in range(fields):
            one, two = carry[f]
            z = coef(2, f, j) * src_ref[f, j] + coef(1, f, j) * two + coef(0, f, j) * one
            z_ref[f, j] = z
            out.append((z, one))
        return tuple(out)

    lax.fori_loop(0, cells, down, tuple((e[0], e[1]) for e in entry), unroll=4)

    def up(i, carry):
        j = cells - 1 - i
        out = []
        for f in range(fields):
            one, two = carry[f]
            v = coef(5, f, j) * z_ref[f, j] + coef(4, f, j) * two + coef(3, f, j) * one
            line_ref[pl.ds(f * rows * cells + j, rows, stride=cells)] = v
            out.append((v, one))
        return tuple(out)

    lax.fori_loop(0, cells, up, tuple((e[2], e[3]) for e in entry), unroll=4)

    for f in range(fields):
        ahead = jnp.zeros((cells, width), f32)
        held = []
        for i in range(rows):
            line = line_ref[pl.ds((f * rows + i) * cells, cells)]
            ahead = rad_ref[(0 * fields + f) * rows + i] * line + rad_ref[(fields + f) * rows + i] * ahead
            held.append(ahead)
        end_ref[f, 0] = ahead
        back = jnp.zeros((cells, width), f32)
        for i in reversed(range(rows)):
            back = rad_ref[(2 * fields + f) * rows + i] * held[i] + rad_ref[(3 * fields + f) * rows + i] * back
        end_ref[f, 1] = back


def third_kernel(enter_ref, rad_ref, *refs):
    ends, (line_ref, out_ref) = refs[:-2], refs[-2:]
    fields, _, cells, width = ends[0].shape
    rows = line_ref.shape[0] // (fields * cells)
    slots = 2 * len(ends)
    for f in range(fields):
        entry = []
        for m in range(2):
            total = jnp.zeros((cells, width), f32)
            for k in range(slots):
                total = total + enter_ref[(m * slots + k) * fields + f] * ends[k // 2][f, k % 2]
            entry.append(total)
        ahead, back = entry
        held = []
        for i in range(rows):
            line = line_ref[pl.ds((f * rows + i) * cells, cells)]
            ahead = rad_ref[(0 * fields + f) * rows + i] * line + rad_ref[(fields + f) * rows + i] * ahead
            held.append(ahead)
        for i in reversed(range(rows)):
            back = rad_ref[(2 * fields + f) * rows + i] * held[i] + rad_ref[(3 * fields + f) * rows + i] * back
            out_ref[pl.ds(f * rows * cells + i, cells, stride=rows)] = back


def azim_table_kernel(coef_ref, enter_ref):
    _, blocks, cells, fields = coef_ref.shape
    own = lax.axis_index("azim")
    unit = lax.broadcasted_iota(jnp.int32, (blocks, 8, fields), 1)

    def ones(k):
        return (unit == k).astype(f32)

    one, two = ones(0), ones(1)
    held = []
    for j in range(cells):
        z = coef_ref[0, :, j : j + 1] * one + coef_ref[1, :, j : j + 1] * two
        held.append(z)
        one, two = z, one
    lower = (one, two)
    one, two = ones(2), ones(3)
    for j in reversed(range(cells)):
        c, e = coef_ref[2, :, j : j + 1], coef_ref[3, :, j : j + 1]
        v = jnp.sqrt(1.0 - (c + e) * (c + e)) * held[j] + c * one + e * two
        one, two = v, one
    upper = (one, two)

    def entry(pair, p, m, k):
        return pair[m][p, k : k + 1]

    count = 4 * blocks
    height = -(-(count + 2) // 8) * 8
    row = lax.broadcasted_iota(jnp.int32, (height, fields), 0)

    def slot(p, k):
        return (row == 4 * (p ^ own) + k).astype(f32)

    def through(order, pair, first, source, start):
        state, entering = start, {}
        for p in order:
            entering[p] = state
            state = tuple(
                source(p, m) + entry(pair, p, m, first) * state[0] + entry(pair, p, m, first + 1) * state[1]
                for m in range(2)
            )
        return state, entering

    def closed(order, pair, first, source):
        start = tuple((row == count + k).astype(f32) for k in range(2))
        (total_one, total_two), _ = through(order, pair, first, source, start)
        a = 1.0 - total_one[count : count + 1]
        b = total_one[count + 1 : count + 2]
        c = total_two[count : count + 1]
        d = 1.0 - total_two[count + 1 : count + 2]
        scale = 1.0 / (a * d - b * c)
        live = row < count
        total_one, total_two = jnp.where(live, total_one, 0.0), jnp.where(live, total_two, 0.0)
        start = ((d * total_one + b * total_two) * scale, (c * total_one + a * total_two) * scale)
        return through(order, pair, first, source, start)[1]

    lower_in = closed(range(blocks), lower, 0, slot)

    def upper_source(p, m):
        z_one, z_two = lower_in[p]
        return slot(p, 2 + m) + entry(upper, p, m, 0) * z_one + entry(upper, p, m, 1) * z_two

    upper_in = closed(list(reversed(range(blocks))), upper, 2, upper_source)
    for m in range(4):
        picked = jnp.zeros((height, fields), f32)
        for p in range(blocks):
            value = lower_in[p][m] if m < 2 else upper_in[p][m - 2]
            picked = jnp.where(own == p, value, picked)
        enter_ref[m] = picked[:count]


def rad_table_kernel(coef_ref, own_ref, enter_ref, pivot_ref):
    _, cells, fields = coef_ref.shape
    rows = own_ref.shape[1]
    blocks = cells // rows
    own = lax.axis_index("rad")
    total = 1.0 + coef_ref[0, 0:1]
    for i in range(cells):
        pivot = coef_ref[1, i : i + 1] + total
        pivot_ref[1 + i : 2 + i] = pivot
        if i + 1 < cells:
            total = 1.0 + coef_ref[0, i + 1 : i + 2] * (total / pivot)
    pivot_ref[0:1] = jnp.ones((1, fields), f32)
    lower, upper = coef_ref[0], coef_ref[1]
    first = lax.broadcasted_iota(jnp.int32, (cells, fields), 0) == 0
    scale = jnp.sqrt(jnp.sqrt(1.0 + lower + upper))
    inverse = 1.0 / pivot_ref[1 : cells + 1]
    forward = jnp.where(first, 0.0, lower / pivot_ref[0:cells])
    backward = upper * inverse
    for kind, table in enumerate((scale, forward, inverse, backward)):
        picked = jnp.zeros((rows, fields), f32)
        for p in range(blocks):
            picked = jnp.where(own == p, table[p * rows : (p + 1) * rows], picked)
        own_ref[kind] = picked

    maps = []
    for p in range(blocks):
        lines = [slice(p * rows + i, p * rows + i + 1) for i in range(rows)]
        ahead, held = jnp.ones((1, fields), f32), []
        for line in lines:
            ahead = forward[line] * ahead
            held.append(ahead)
        back, gain = jnp.zeros((1, fields), f32), jnp.ones((1, fields), f32)
        for line, value in zip(reversed(lines), reversed(held)):
            back = inverse[line] * value + backward[line] * back
            gain = backward[line] * gain
        maps.append((ahead, back, gain))
    count = 2 * blocks
    height = -(-count // 8) * 8
    row = lax.broadcasted_iota(jnp.int32, (height, fields), 0)

    def slot(p, k):
        return (row == 2 * (p ^ own) + k).astype(f32)

    zero = jnp.zeros((height, fields), f32)
    ahead, ahead_in = zero, {}
    for p in range(blocks):
        ahead_in[p] = ahead
        ahead = slot(p, 0) + maps[p][0] * ahead
    back, back_in = zero, {}
    for p in reversed(range(blocks)):
        back_in[p] = back
        back = slot(p, 1) + maps[p][1] * ahead_in[p] + maps[p][2] * back
    for m, entering in enumerate((ahead_in, back_in)):
        picked = zero
        for p in range(blocks):
            picked = jnp.where(own == p, entering[p], picked)
        enter_ref[m] = picked[:count]


def from_partners(values, axis):
    count = lax.axis_size(axis)
    return [values] + [
        lax.ppermute(values, axis, [(i, i ^ s) for i in range(count)]) for s in range(1, count)
    ]


def local(residual, left_vec, dissip, azim_coef, radial_coef):
    fields, cells, rows, width = residual.shape
    azim_count, rad_count = lax.axis_size("azim"), lax.axis_size("rad")
    edge = call(edge_kernel, [(fields, rows, width)], 0, 1)(residual)[0]
    halo = lax.ppermute(edge, "axial", [(0, 1), (1, 0)])

    weights = jnp.sqrt(1.0 - (azim_coef[0::2] + azim_coef[1::2]) ** 2)
    kinds = jnp.concatenate([azim_coef[:2], weights[:1], azim_coef[2:], weights[1:]])
    own_azim = lax.dynamic_slice_in_dim(kinds, lax.axis_index("azim") * cells, cells, 2).reshape(-1)
    azim_blocks = azim_coef.reshape(4, fields, azim_count, cells).transpose(0, 2, 3, 1)
    azim_enter = call(azim_table_kernel, [(4, 4 * azim_count, fields)], 0, 1)(azim_blocks)[0].reshape(-1)
    all_rows = rad_count * rows
    own_rad, rad_enter = call(
        rad_table_kernel,
        [(4, rows, fields), (2, 2 * rad_count, fields)],
        0,
        1,
        [(all_rows + 8, fields)],
    )(radial_coef.transpose(0, 2, 1))
    own_rad, rad_enter = own_rad.transpose(0, 2, 1).reshape(-1), rad_enter.reshape(-1)

    whole = (fields, cells, rows, width)
    src, states = call(first_kernel, [whole, (fields, 4, rows, width)], 3, 2, [whole])(
        own_azim, left_vec.reshape(-1), dissip, residual, halo
    )
    gathered = from_partners(states, "azim")
    flat = (fields * cells * rows, width)
    lines, ends = call(second_kernel, [flat, (fields, 2, cells, width)], 3, 1 + azim_count, [whole])(
        own_azim, azim_enter, own_rad, *gathered, src
    )
    gathered = from_partners(ends, "rad")
    out = call(third_kernel, [flat], 2, 1 + rad_count)(rad_enter, own_rad, *gathered, lines)[0]
    return out.reshape(whole)


def solution(mesh):
    placed = (P(None, "azim", "rad", "axial"), P(), P(), P(), P())
    return jax.shard_map(
        local,
        mesh=mesh,
        in_specs=placed,
        out_specs=P(None, "azim", "rad", "axial"),
        check_vma=False,
    )
```

```python
import jax
import jax.numpy as jnp
from jax import lax
from jax.experimental import pallas as pl
from jax.experimental.pallas import tpu as pltpu
from jax.sharding import PartitionSpec as P

f32 = jnp.float32
VMEM = pl.BlockSpec(memory_space=pltpu.VMEM)
SMEM = pl.BlockSpec(memory_space=pltpu.SMEM)
params = pltpu.CompilerParams(vmem_limit_bytes=32 * 1024 * 1024)


def call(body, outs, n_smem, n_vmem, scratch=()):
    return pl.pallas_call(
        body,
        out_shape=[jax.ShapeDtypeStruct(shape, f32) for shape in outs],
        in_specs=[SMEM] * n_smem + [VMEM] * n_vmem,
        out_specs=[VMEM] * len(outs),
        scratch_shapes=[pltpu.VMEM(shape, f32) for shape in scratch],
        compiler_params=params,
    )


def lanes_of(shape):
    return lax.broadcasted_iota(jnp.int32, shape, len(shape) - 1)


def low_high(count):
    split = 1 << ((count.bit_length() - 1) // 2)
    return list(range(split)), list(range(0, count, split))


def targets_of(count):
    low, high = low_high(count)
    return low + high[1:]


def far_lane(width):
    return jnp.where(lax.axis_index("axial") == 0, width - 1, 0)


def edge_kernel(res_ref, edge_ref):
    fields, cells, rows, width = res_ref.shape
    source = far_lane(width)
    lane = lanes_of((rows, width))

    def step(j, packed):
        return tuple(
            jnp.where(lane == j, pltpu.roll(res_ref[f, j], (j - source + width) % width, 1), packed[f])
            for f in range(fields)
        )

    edge_ref[...] = jnp.zeros(edge_ref.shape, f32)
    packed = lax.fori_loop(0, cells, step, tuple(edge_ref[f] for f in range(fields)), unroll=4)
    for f in range(fields):
        edge_ref[f] = packed[f]


def lower_sweep(coef_ref, cells, load, z_ref, start):
    fields = len(start)

    def step(j, carry):
        source = load(j)
        out = []
        for f in range(fields):
            one, two = carry[f]
            at = f * cells + j
            z = (
                coef_ref[2 * fields * cells + at] * source[f]
                + coef_ref[fields * cells + at] * two
                + coef_ref[at] * one
            )
            z_ref[f, j] = z
            out.append((z, one))
        return tuple(out)

    return lax.fori_loop(0, cells, step, start, unroll=4)


def upper_sweep(coef_ref, cells, z_ref, start, store=None):
    fields = len(start)

    def step(i, carry):
        j = cells - 1 - i
        out = []
        for f in range(fields):
            one, two = carry[f]
            at = f * cells + j
            v = (
                coef_ref[5 * fields * cells + at] * z_ref[f, j]
                + coef_ref[4 * fields * cells + at] * two
                + coef_ref[3 * fields * cells + at] * one
            )
            if store is not None:
                store(f, j, v)
            out.append((v, one))
        return tuple(out)

    return lax.fori_loop(0, cells, step, start, unroll=4)


def radial_sweeps(rad_ref, fields, rows, f, load, ahead, back, store=None):
    def coef(kind, i):
        return rad_ref[(kind * fields + f) * rows + i]

    held = []
    for i in range(rows):
        line = coef(0, i) * load(i)
        ahead = line if ahead is None else line + coef(1, i) * ahead
        held.append(ahead)
    for i in reversed(range(rows)):
        line = coef(2, i) * held[i]
        back = line if back is None else line + coef(3, i) * back
        if store is not None:
            store(i, back)
    return ahead, back


def mix(vec_ref, values):
    fields = len(values)
    return [sum(vec_ref[g * fields + f] * values[f] for f in range(fields)) for g in range(fields)]


def first_kernel(coef_ref, vec_ref, dis_ref, res_ref, src_ref, state_ref, z_ref):
    fields, cells, rows, width = res_ref.shape
    lane = lanes_of((rows, width))

    def load(j):
        out = []
        for f, c in enumerate(mix(vec_ref, [res_ref[f, j] for f in range(fields)])):
            beside = jnp.where(lane == 0, 0.0, pltpu.roll(c, 1, 1)) + jnp.where(
                lane == width - 1, 0.0, pltpu.roll(c, width - 1, 1)
            )
            src = (1.0 - 2.0 * dis_ref[f]) * c + dis_ref[f] * beside
            src_ref[f, j] = src
            out.append(src)
        return out

    state_ref[...] = jnp.zeros(state_ref.shape, f32)
    start = tuple((state_ref[f, 0], state_ref[f, 1]) for f in range(fields))
    carry = lower_sweep(coef_ref, cells, load, z_ref, start)
    for f in range(fields):
        state_ref[f, 0], state_ref[f, 1] = carry[f]
    start = tuple((state_ref[f, 2], state_ref[f, 3]) for f in range(fields))
    carry = upper_sweep(coef_ref, cells, z_ref, start)
    for f in range(fields):
        state_ref[f, 2], state_ref[f, 3] = carry[f]


def patch_kernel(vec_ref, dis_ref, rad_ref, halo_ref, state_ref, reply_ref, out_ref, part_ref, end_ref):
    fields, _, rows, width = state_ref.shape
    lane = lanes_of((rows, width))
    target = far_lane(width)
    for f, h in enumerate(mix(vec_ref, [halo_ref[f] for f in range(fields)])):
        h = dis_ref[f] * h
        part_ref[f] = h
        for m in range(4):
            extra = jnp.sum(h * reply_ref[f, m : m + 1], axis=1, keepdims=True)
            out_ref[pl.ds((f * 4 + m) * rows, rows)] = state_ref[f, m] + jnp.where(lane == target, extra, 0.0)
    for f in range(fields):
        ahead, back = radial_sweeps(
            rad_ref, fields, rows, f, lambda i: out_ref[pl.ds(f * 4 * rows + i, 4, stride=rows)], None, None
        )
        end_ref[f, 0:4] = ahead
        end_ref[f, 4:8] = back


def source_kernel(rad_ref, src_ref, part_ref, out_ref, end_ref):
    fields, cells, rows, width = src_ref.shape
    lane = lanes_of((rows, width))
    target = far_lane(width)

    def step(j, carry):
        for f in range(fields):
            moved = pltpu.roll(part_ref[f], (target - j + width) % width, 1)
            tile = src_ref[f, j] + jnp.where(lane == target, moved, 0.0)
            out_ref[pl.ds(pl.multiple_of((f * cells + j) * rows, rows), rows)] = tile
        return carry

    lax.fori_loop(0, cells, step, 0, unroll=2)
    for f in range(fields):
        end_ref[f, 0], end_ref[f, 1] = radial_sweeps(
            rad_ref, fields, rows, f, lambda i: out_ref[pl.ds(f * cells * rows + i, cells, stride=rows)], None, None
        )


def weighted(enter_ref, fields, f, width, target, m, pieces):
    total = None
    for column, value in pieces:
        term = enter_ref[((target[0] * target[1] + m) * width + column) * fields + f] * value
        total = term if total is None else total + term
    return total


def state_kernel(rad_enter_ref, rad_ref, *refs):
    ends, (state_ref, first_ref, second_ref, work_ref) = refs[:-4], refs[-4:]
    fields, _, half, width = first_ref.shape
    rows = 2 * half
    for f in range(fields):
        pieces = [(2 * s + k, ends[s][f, 4 * k : 4 * k + 4]) for s in range(len(ends)) for k in range(2)]
        ahead, back = (
            weighted(rad_enter_ref, fields, f, 2 * len(ends), (0, 2), m, pieces) for m in range(2)
        )

        def store(i, value):
            work_ref[pl.ds(f * 4 * rows + i, 4, stride=rows)] = value

        radial_sweeps(
            rad_ref, fields, rows, f, lambda i: state_ref[pl.ds(f * 4 * rows + i, 4, stride=rows)], ahead, back, store
        )
        for m in range(4):
            at = (f * 4 + m) * rows
            first_ref[f, m] = work_ref[pl.ds(at, half)]
            second_ref[f, m] = work_ref[pl.ds(at + half, half)]


def spread_kernel(count, size, near, far, enter_ref, *refs):
    arrays, sums = refs[: len(near)], refs[len(near) :]
    fields = sums[0].shape[0]
    for s, out_ref in zip(far, sums):
        target = targets_of(count).index(s)
        for f in range(fields):
            pieces = [(size * n + k, ref[f, k]) for n, ref in zip(near, arrays) for k in range(size)]
            for m in range(size):
                out_ref[f, m] = weighted(enter_ref, fields, f, size * count, (target, size), m, pieces)


def spread_both(count, near, far, enter_ref, *refs):
    ins, outs = refs[: len(near) + len(far)], refs[len(near) + len(far) :]
    spread_kernel(count, 4, near, far, enter_ref, *ins[: len(near)], *outs[: len(far)])
    spread_kernel(count, 4, far, near, enter_ref, *ins[len(near) :], *outs[len(far) :])


def radial_kernel(rad_ref, *refs):
    ends, (src_ref, out_ref) = refs[:-2], refs[-2:]
    fields, _, cells, width = ends[0].shape
    rows = src_ref.shape[0] // (fields * cells)
    for f in range(fields):
        ahead, back = (sum(ref[f, m] for ref in ends) for m in range(2))

        def store(i, value):
            out_ref[pl.ds(f * cells * rows + i, cells, stride=rows)] = value

        radial_sweeps(
            rad_ref,
            fields,
            rows,
            f,
            lambda i: src_ref[pl.ds(f * cells * rows + i, cells, stride=rows)],
            ahead,
            back,
            store,
        )


def last_kernel(coef_ref, *refs):
    parts, (src_ref, out_ref, z_ref) = refs[:-3], refs[-3:]
    count = len(parts) // 2
    fields, cells, rows, width = src_ref.shape
    entry = [
        [
            jnp.concatenate([sum(ref[f, m] for ref in parts[:count]), sum(ref[f, m] for ref in parts[count:])])
            for m in range(4)
        ]
        for f in range(fields)
    ]
    lower_sweep(
        coef_ref,
        cells,
        lambda j: [src_ref[f, j] for f in range(fields)],
        z_ref,
        tuple((e[0], e[1]) for e in entry),
    )

    def store(f, j, value):
        out_ref[f, j] = value

    upper_sweep(coef_ref, cells, z_ref, tuple((e[2], e[3]) for e in entry), store)


def azim_table_kernel(coef_ref, enter_ref, reply_ref):
    _, blocks, cells, fields = coef_ref.shape
    own = lax.axis_index("azim")

    def weight(a, b):
        return jnp.sqrt(1.0 - (a + b) * (a + b))

    unit = lax.broadcasted_iota(jnp.int32, (blocks, 8, fields), 1)

    def ones(k):
        return (unit == k).astype(f32)

    one, two = ones(0), ones(1)
    held = []
    for j in range(cells):
        z = coef_ref[0, :, j : j + 1] * one + coef_ref[1, :, j : j + 1] * two
        held.append(z)
        one, two = z, one
    lower = (one, two)
    one, two = ones(2), ones(3)
    for j in reversed(range(cells)):
        c, e = coef_ref[2, :, j : j + 1], coef_ref[3, :, j : j + 1]
        v = weight(c, e) * held[j] + c * one + e * two
        one, two = v, one
    upper = (one, two)

    cell = lax.broadcasted_iota(jnp.int32, (cells, fields), 0)
    one = two = jnp.zeros((cells, fields), f32)
    held = []
    for j in range(cells):
        a, b = coef_ref[0, own, j : j + 1], coef_ref[1, own, j : j + 1]
        z = jnp.where(cell == j, weight(a, b), 0.0) + a * one + b * two
        held.append(z)
        one, two = z, one
    reply_ref[0], reply_ref[1] = one, two
    one = two = jnp.zeros((cells, fields), f32)
    for j in reversed(range(cells)):
        c, e = coef_ref[2, own, j : j + 1], coef_ref[3, own, j : j + 1]
        v = weight(c, e) * held[j] + c * one + e * two
        one, two = v, one
    reply_ref[2], reply_ref[3] = one, two

    def entry(pair, p, m, k):
        return pair[m][p, k : k + 1]

    count = 4 * blocks
    height = -(-(count + 2) // 8) * 8
    row = lax.broadcasted_iota(jnp.int32, (height, fields), 0)

    def slot(p, k):
        return (row == 4 * (p ^ own) + k).astype(f32)

    def through(order, pair, first, source, start):
        state, entering = start, {}
        for p in order:
            entering[p] = state
            state = tuple(
                source(p, m) + entry(pair, p, m, first) * state[0] + entry(pair, p, m, first + 1) * state[1]
                for m in range(2)
            )
        return state, entering

    def closed(order, pair, first, source):
        start = tuple((row == count + k).astype(f32) for k in range(2))
        (total_one, total_two), _ = through(order, pair, first, source, start)
        a = 1.0 - total_one[count : count + 1]
        b = total_one[count + 1 : count + 2]
        c = total_two[count : count + 1]
        d = 1.0 - total_two[count + 1 : count + 2]
        scale = 1.0 / (a * d - b * c)
        live = row < count
        total_one, total_two = jnp.where(live, total_one, 0.0), jnp.where(live, total_two, 0.0)
        start = ((d * total_one + b * total_two) * scale, (c * total_one + a * total_two) * scale)
        return through(order, pair, first, source, start)[1]

    lower_in = closed(range(blocks), lower, 0, slot)

    def upper_source(p, m):
        z_one, z_two = lower_in[p]
        return slot(p, 2 + m) + entry(upper, p, m, 0) * z_one + entry(upper, p, m, 1) * z_two

    upper_in = closed(list(reversed(range(blocks))), upper, 2, upper_source)
    for i, step in enumerate(targets_of(blocks)):
        for m in range(4):
            picked = jnp.zeros((height, fields), f32)
            for p in range(blocks):
                value = lower_in[p][m] if m < 2 else upper_in[p][m - 2]
                picked = jnp.where(own == (p ^ step), value, picked)
            enter_ref[i, m] = picked[:count]


def rad_table_kernel(coef_ref, own_ref, enter_ref, pivot_ref):
    _, cells, fields = coef_ref.shape
    rows = own_ref.shape[1]
    blocks = cells // rows
    own = lax.axis_index("rad")
    total = 1.0 + coef_ref[0, 0:1]
    for i in range(cells):
        pivot = coef_ref[1, i : i + 1] + total
        pivot_ref[1 + i : 2 + i] = pivot
        if i + 1 < cells:
            total = 1.0 + coef_ref[0, i + 1 : i + 2] * (total / pivot)
    pivot_ref[0:1] = jnp.ones((1, fields), f32)
    lower, upper = coef_ref[0], coef_ref[1]
    first = lax.broadcasted_iota(jnp.int32, (cells, fields), 0) == 0
    scale = jnp.sqrt(jnp.sqrt(1.0 + lower + upper))
    inverse = 1.0 / pivot_ref[1 : cells + 1]
    forward = jnp.where(first, 0.0, lower / pivot_ref[0:cells])
    backward = upper * inverse
    for kind, table in enumerate((scale, forward, inverse, backward)):
        picked = jnp.zeros((rows, fields), f32)
        for p in range(blocks):
            picked = jnp.where(own == p, table[p * rows : (p + 1) * rows], picked)
        own_ref[kind] = picked

    maps = []
    for p in range(blocks):
        lines = [slice(p * rows + i, p * rows + i + 1) for i in range(rows)]
        ahead, held = jnp.ones((1, fields), f32), []
        for line in lines:
            ahead = forward[line] * ahead
            held.append(ahead)
        back, gain = jnp.zeros((1, fields), f32), jnp.ones((1, fields), f32)
        for line, value in zip(reversed(lines), reversed(held)):
            back = inverse[line] * value + backward[line] * back
            gain = backward[line] * gain
        maps.append((ahead, back, gain))
    count = 2 * blocks
    height = -(-count // 8) * 8
    row = lax.broadcasted_iota(jnp.int32, (height, fields), 0)

    def slot(p, k):
        return (row == 2 * (p ^ own) + k).astype(f32)

    zero = jnp.zeros((height, fields), f32)
    ahead, ahead_in = zero, {}
    for p in range(blocks):
        ahead_in[p] = ahead
        ahead = slot(p, 0) + maps[p][0] * ahead
    back, back_in = zero, {}
    for p in reversed(range(blocks)):
        back_in[p] = back
        back = slot(p, 1) + maps[p][1] * ahead_in[p] + maps[p][2] * back
    for i, step in enumerate(targets_of(blocks)):
        for m, entering in enumerate((ahead_in, back_in)):
            picked = zero
            for p in range(blocks):
                picked = jnp.where(own == (p ^ step), entering[p], picked)
            enter_ref[i, m] = picked[:count]


def from_partner(values, axis, step):
    if step == 0:
        return values
    return lax.ppermute(values, axis, [(i, i ^ step) for i in range(lax.axis_size(axis))])


def local(residual, left_vec, dissip, azim_coef, radial_coef):
    fields, cells, rows, width = residual.shape
    azim_count, rad_count = lax.axis_size("azim"), lax.axis_size("rad")
    whole, flat = (fields, cells, rows, width), (fields * cells * rows, width)
    edge = call(edge_kernel, [(fields, rows, width)], 0, 1)(residual)[0]
    halo = lax.ppermute(edge, "axial", [(0, 1), (1, 0)])

    weights = jnp.sqrt(1.0 - (azim_coef[0::2] + azim_coef[1::2]) ** 2)
    kinds = jnp.concatenate([azim_coef[:2], weights[:1], azim_coef[2:], weights[1:]])
    own_azim = lax.dynamic_slice_in_dim(kinds, lax.axis_index("azim") * cells, cells, 2).reshape(-1)
    azim_blocks = azim_coef.reshape(4, fields, azim_count, cells).transpose(0, 2, 3, 1)
    azim_enter, reply = call(
        azim_table_kernel,
        [(len(targets_of(azim_count)), 4, 4 * azim_count, fields), (4, cells, fields)],
        0,
        1,
    )(azim_blocks)
    reply = jnp.pad(reply.transpose(2, 0, 1), ((0, 0), (0, 0), (0, width - cells)))
    own_rad, rad_enter = call(
        rad_table_kernel,
        [(4, rows, fields), (len(targets_of(rad_count)), 2, 2 * rad_count, fields)],
        0,
        1,
        [(rad_count * rows + 8, fields)],
    )(radial_coef.transpose(0, 2, 1))
    azim_enter, rad_enter = azim_enter.reshape(-1), rad_enter.reshape(-1)
    own_rad = own_rad.transpose(0, 2, 1).reshape(-1)
    vec = left_vec.reshape(-1)

    four = (fields, 4, rows, width)
    src, states = call(first_kernel, [whole, four], 3, 1, [whole])(own_azim, vec, dissip, residual)
    states, part, small = call(
        patch_kernel, [(fields * 4 * rows, width), (fields, rows, width), (fields, 8, width)], 3, 3
    )(vec, dissip, own_rad, halo, states, reply)
    smalls = [from_partner(small, "rad", s) for s in range(rad_count)]
    src, ends = call(source_kernel, [flat, (fields, 2, cells, width)], 1, 2)(own_rad, src, part)
    half = (fields, 4, rows // 2, width)
    one, two = call(state_kernel, [half, half], 2, rad_count + 1, [(fields * 4 * rows, width)])(
        rad_enter, own_rad, *smalls, states
    )
    low, high = low_high(azim_count)
    ones = [from_partner(one, "azim", s) for s in low]
    twos = [from_partner(two, "azim", s) for s in high]

    near, far = low_high(rad_count)
    gathered = [from_partner(ends, "rad", s) for s in near]
    sums = call(
        lambda *refs: spread_kernel(rad_count, 2, near, far, *refs), [ends.shape] * len(far), 1, len(near)
    )(rad_enter, *gathered)
    entry = [from_partner(value, "rad", s) for s, value in zip(far, sums)]
    src = call(radial_kernel, [flat], 1, len(far) + 1)(own_rad, *entry, src)[0]

    sums = call(
        lambda *refs: spread_both(azim_count, low, high, *refs),
        [half] * (len(low) + len(high)),
        1,
        len(low) + len(high),
    )(azim_enter, *ones, *twos)
    ones = [from_partner(value, "azim", s) for s, value in zip(high, sums[: len(high)])]
    twos = [from_partner(value, "azim", s) for s, value in zip(low, sums[len(high) :])]
    ones = ones + [jnp.zeros_like(one)] * (max(len(low), len(high)) - len(high))
    twos = twos + [jnp.zeros_like(two)] * (max(len(low), len(high)) - len(low))
    return call(last_kernel, [whole], 1, len(ones) + len(twos) + 1, [whole])(
        own_azim, *ones, *twos, src.reshape(whole)
    )[0]


def solution(mesh):
    placed = (P(None, "azim", "rad", "axial"), P(), P(), P(), P())
    return jax.shard_map(
        local,
        mesh=mesh,
        in_specs=placed,
        out_specs=P(None, "azim", "rad", "axial"),
        check_vma=False,
    )
```

```python
import jax
import jax.numpy as jnp
from jax import lax
from jax.experimental import pallas as pl
from jax.experimental.pallas import tpu as pltpu
from jax.sharding import PartitionSpec as P

f32 = jnp.float32
VMEM = pl.BlockSpec(memory_space=pltpu.VMEM)
SMEM = pl.BlockSpec(memory_space=pltpu.SMEM)
params = pltpu.CompilerParams(vmem_limit_bytes=32 * 1024 * 1024)


def call(body, outs, n_smem, n_vmem, scratch=(), cost=0):
    return pl.pallas_call(
        body,
        out_shape=[jax.ShapeDtypeStruct(shape, f32) for shape in outs],
        in_specs=[SMEM] * n_smem + [VMEM] * n_vmem,
        out_specs=[VMEM] * len(outs),
        scratch_shapes=[pltpu.VMEM(shape, f32) for shape in scratch],
        compiler_params=params,
        cost_estimate=pl.CostEstimate(flops=cost, bytes_accessed=0, transcendentals=0),
    )


def lanes_of(shape):
    return lax.broadcasted_iota(jnp.int32, shape, len(shape) - 1)


def low_high(count):
    split = 1 << ((count.bit_length() - 1) // 2)
    return list(range(split)), list(range(0, count, split))


def targets_of(count):
    low, high = low_high(count)
    return low + high[1:]


def far_lane(width):
    return jnp.where(lax.axis_index("axial") == 0, width - 1, 0)


def edge_kernel(res_ref, edge_ref):
    fields, cells, rows, width = res_ref.shape
    source = far_lane(width)
    lane = lanes_of((rows, width))
    packed = [jnp.zeros((rows, width), f32)] * fields
    for j in range(cells):
        for f in range(fields):
            moved = pltpu.roll(res_ref[f, j], (j - source + width) % width, 1)
            packed[f] = jnp.where(lane == j, moved, packed[f])
    for f in range(fields):
        edge_ref[f] = packed[f]


def lower_sweep(coef_ref, cells, load, z_ref, start):
    fields = len(start)

    def step(j, carry):
        source = load(j)
        out = []
        for f in range(fields):
            one, two = carry[f]
            at = f * cells + j
            z = (
                coef_ref[2 * fields * cells + at] * source[f]
                + coef_ref[fields * cells + at] * two
                + coef_ref[at] * one
            )
            z_ref[f, j] = z
            out.append((z, one))
        return tuple(out)

    return lax.fori_loop(0, cells, step, start, unroll=4)


def upper_sweep(coef_ref, cells, z_ref, start, store=None, first=0, count=None):
    fields = len(start)
    count = cells if count is None else count

    def step(i, carry):
        j = first + count - 1 - i
        out = []
        for f in range(fields):
            one, two = carry[f]
            at = f * cells + j
            v = (
                coef_ref[5 * fields * cells + at] * z_ref[f, j]
                + coef_ref[4 * fields * cells + at] * two
                + coef_ref[3 * fields * cells + at] * one
            )
            if store is not None:
                store(f, j, v)
            out.append((v, one))
        return tuple(out)

    return lax.fori_loop(0, count, step, start, unroll=4)


def radial_sweeps(rad_ref, fields, rows, f, load, ahead, back, store=None):
    def coef(kind, i):
        return rad_ref[(kind * fields + f) * rows + i]

    held = []
    for i in range(rows):
        line = coef(0, i) * load(i)
        ahead = line if ahead is None else line + coef(1, i) * ahead
        held.append(ahead)
    for i in reversed(range(rows)):
        line = coef(2, i) * held[i]
        back = line if back is None else line + coef(3, i) * back
        if store is not None:
            store(i, back)
    return ahead, back


def mix(vec_ref, values):
    fields = len(values)
    return [sum(vec_ref[g * fields + f] * values[f] for f in range(fields)) for g in range(fields)]


def first_kernel(coef_ref, vec_ref, dis_ref, res_ref, src_ref, state_ref, z_ref):
    fields, cells, rows, width = res_ref.shape
    lane = lanes_of((rows, width))

    def load(j):
        out = []
        for f, c in enumerate(mix(vec_ref, [res_ref[f, j] for f in range(fields)])):
            beside = jnp.where(lane == 0, 0.0, pltpu.roll(c, 1, 1)) + jnp.where(
                lane == width - 1, 0.0, pltpu.roll(c, width - 1, 1)
            )
            src = (1.0 - 2.0 * dis_ref[f]) * c + dis_ref[f] * beside
            src_ref[f, j] = src
            out.append(src)
        return out

    state_ref[...] = jnp.zeros(state_ref.shape, f32)
    start = tuple((state_ref[f, 0], state_ref[f, 1]) for f in range(fields))
    carry = lower_sweep(coef_ref, cells, load, z_ref, start)
    for f in range(fields):
        state_ref[f, 0], state_ref[f, 1] = carry[f]
    start = tuple((state_ref[f, 2], state_ref[f, 3]) for f in range(fields))
    carry = upper_sweep(coef_ref, cells, z_ref, start)
    for f in range(fields):
        state_ref[f, 2], state_ref[f, 3] = carry[f]


def patch_kernel(
    vec_ref, dis_ref, rad_ref, halo_ref, state_ref, reply_ref, first_ref, second_ref, part_ref, end_ref, work_ref
):
    fields, _, rows, width = state_ref.shape
    lane = lanes_of((rows, width))
    target = far_lane(width)
    for f, h in enumerate(mix(vec_ref, [halo_ref[f] for f in range(fields)])):
        h = dis_ref[f] * h
        part_ref[f] = h
        for m in range(4):
            extra = jnp.sum(h * reply_ref[f, m : m + 1], axis=1, keepdims=True)
            tile = state_ref[f, m] + jnp.where(lane == target, extra, 0.0)
            first_ref[f, m] = tile[: rows // 2]
            second_ref[f, m] = tile[rows // 2 :]
            work_ref[pl.ds((f * 4 + m) * rows, rows)] = tile
    for f in range(fields):
        ahead, back = radial_sweeps(
            rad_ref, fields, rows, f, lambda i: work_ref[pl.ds(f * 4 * rows + i, 4, stride=rows)], None, None
        )
        end_ref[f, 0:4] = ahead
        end_ref[f, 4:8] = back


def source_kernel(rad_ref, src_ref, part_ref, out_ref, end_ref):
    fields, cells, rows, width = src_ref.shape
    lane = lanes_of((rows, width))
    target = far_lane(width)

    def step(j, carry):
        for f in range(fields):
            moved = pltpu.roll(part_ref[f], (target - j + width) % width, 1)
            tile = src_ref[f, j] + jnp.where(lane == target, moved, 0.0)
            out_ref[pl.ds(pl.multiple_of((f * cells + j) * rows, rows), rows)] = tile
        return carry

    lax.fori_loop(0, cells, step, 0, unroll=8)
    for f in range(fields):
        end_ref[f, 0], end_ref[f, 1] = radial_sweeps(
            rad_ref, fields, rows, f, lambda i: out_ref[pl.ds(f * cells * rows + i, cells, stride=rows)], None, None
        )


def weighted(enter_ref, fields, f, width, target, m, pieces):
    total = None
    for column, value in pieces:
        term = enter_ref[((target[0] * target[1] + m) * width + column) * fields + f] * value
        total = term if total is None else total + term
    return total


def spread_kernel(count, size, near, far, enter_ref, *refs):
    arrays, sums = refs[: len(near)], refs[len(near) :]
    fields = sums[0].shape[0]
    for s, out_ref in zip(far, sums):
        target = targets_of(count).index(s)
        for f in range(fields):
            pieces = [(size * n + k, ref[f, k]) for n, ref in zip(near, arrays) for k in range(size)]
            for m in range(size):
                out_ref[f, m] = weighted(enter_ref, fields, f, size * count, (target, size), m, pieces)


def send_kernel(count, near, far, rads, enter_ref, rad_enter_ref, *refs):
    firsts, refs = refs[: len(near)], refs[len(near) :]
    seconds, refs = refs[: len(far)], refs[len(far) :]
    ends, outs = refs[:rads], refs[rads:]
    fields = ends[0].shape[0]
    spread_kernel(count, 4, near, far, enter_ref, *firsts, *outs[: len(far)])
    spread_kernel(count, 4, far, near, enter_ref, *seconds, *outs[len(far) : -1])
    for f in range(fields):
        pieces = [(2 * s + k, ends[s][f, 4 * k : 4 * k + 4]) for s in range(rads) for k in range(2)]
        for m in range(2):
            own = weighted(rad_enter_ref, fields, f, 2 * rads, (0, 2), m, pieces)
            for out_ref in outs[:-1]:
                out_ref[f, 4, 4 * m : 4 * m + 4] = own
            outs[-1][f, 4 * m : 4 * m + 4] = own


def radial_kernel(rad_ref, *refs):
    ends, (src_ref, out_ref) = refs[:-2], refs[-2:]
    fields, _, cells, width = ends[0].shape
    rows = src_ref.shape[0] // (fields * cells)
    for f in range(fields):
        ahead, back = (sum(ref[f, m] for ref in ends) for m in range(2))

        def store(i, value):
            out_ref[pl.ds(f * cells * rows + i, cells, stride=rows)] = value

        radial_sweeps(
            rad_ref,
            fields,
            rows,
            f,
            lambda i: src_ref[pl.ds(f * cells * rows + i, cells, stride=rows)],
            ahead,
            back,
            store,
        )


def last_kernel(firsts, seconds, steps, coef_ref, enter_ref, rad_ref, *refs):
    parts, (src_ref, out_ref, z_ref, work_ref, held_ref, sems) = refs[:-6], refs[-6:]
    fields, cells, rows, width = src_ref.shape
    half = rows // 2
    at = {s: i for i, s in reversed(list(enumerate(steps)))}
    entry = []
    for f in range(fields):
        for m in range(4):
            base = (f * 4 + m) * rows
            work_ref[pl.ds(base, half)] = sum(ref[f, m] for ref in parts[:firsts])
            work_ref[pl.ds(base + half, half)] = sum(ref[f, m] for ref in parts[firsts : firsts + seconds])

        def row(s, k):
            ref = parts[at[s]]
            if at[s] < firsts + seconds:
                return ref[f, 4, k : k + 1]
            return ref[f, k : k + 1]

        sides = [
            jnp.concatenate(
                [
                    weighted(
                        enter_ref,
                        fields,
                        f,
                        4 * len(at),
                        (0, 4),
                        m,
                        [(4 * s + k, row(s, 4 * side + k)) for s in range(len(at)) for k in range(4)],
                    )
                    for m in range(4)
                ]
            )
            for side in range(2)
        ]

        def store(i, value):
            work_ref[pl.ds(f * 4 * rows + i, 4, stride=rows)] = value

        radial_sweeps(
            rad_ref, fields, rows, f, lambda i: work_ref[pl.ds(f * 4 * rows + i, 4, stride=rows)], *sides, store
        )
        entry.append([work_ref[pl.ds((f * 4 + m) * rows, rows)] for m in range(4)])
    lower_sweep(
        coef_ref,
        cells,
        lambda j: [src_ref[f, j] for f in range(fields)],
        z_ref,
        tuple((e[0], e[1]) for e in entry),
    )

    def store(f, j, value):
        held_ref[f, j] = value

    chunks = sems.shape[0]
    size = cells // chunks
    carry = tuple((e[2], e[3]) for e in entry)
    copies = []
    for c in reversed(range(chunks)):
        carry = upper_sweep(coef_ref, cells, z_ref, carry, store, c * size, size)
        copies.append(
            pltpu.make_async_copy(
                held_ref.at[:, pl.ds(c * size, size)], out_ref.at[:, pl.ds(c * size, size)], sems.at[c]
            )
        )
        copies[-1].start()
    for copy in copies:
        copy.wait()


def weight(a, b):
    return jnp.sqrt(1.0 - (a + b) * (a + b))


def reply_kernel(coef_ref, reply_ref):
    _, blocks, cells, fields = coef_ref.shape
    own = lax.axis_index("azim")
    cell = lax.broadcasted_iota(jnp.int32, (cells, fields), 0)
    one = two = jnp.zeros((cells, fields), f32)
    held = []
    for j in range(cells):
        a, b = coef_ref[0, own, j : j + 1], coef_ref[1, own, j : j + 1]
        z = jnp.where(cell == j, weight(a, b), 0.0) + a * one + b * two
        held.append(z)
        one, two = z, one
    reply_ref[0], reply_ref[1] = one, two
    one = two = jnp.zeros((cells, fields), f32)
    for j in reversed(range(cells)):
        c, e = coef_ref[2, own, j : j + 1], coef_ref[3, own, j : j + 1]
        v = weight(c, e) * held[j] + c * one + e * two
        one, two = v, one
    reply_ref[2], reply_ref[3] = one, two


def azim_table_kernel(coef_ref, enter_ref):
    _, blocks, cells, fields = coef_ref.shape
    own = lax.axis_index("azim")
    unit = lax.broadcasted_iota(jnp.int32, (blocks, 8, fields), 1)

    def ones(k):
        return (unit == k).astype(f32)

    one, two = ones(0), ones(1)
    held = []
    for j in range(cells):
        z = coef_ref[0, :, j : j + 1] * one + coef_ref[1, :, j : j + 1] * two
        held.append(z)
        one, two = z, one
    lower = (one, two)
    one, two = ones(2), ones(3)
    for j in reversed(range(cells)):
        c, e = coef_ref[2, :, j : j + 1], coef_ref[3, :, j : j + 1]
        v = weight(c, e) * held[j] + c * one + e * two
        one, two = v, one
    upper = (one, two)

    def entry(pair, p, m, k):
        return pair[m][p, k : k + 1]

    count = 4 * blocks
    height = -(-(count + 2) // 8) * 8
    row = lax.broadcasted_iota(jnp.int32, (height, fields), 0)

    def slot(p, k):
        return (row == 4 * (p ^ own) + k).astype(f32)

    def through(order, pair, first, source, start):
        state, entering = start, {}
        for p in order:
            entering[p] = state
            state = tuple(
                source(p, m) + entry(pair, p, m, first) * state[0] + entry(pair, p, m, first + 1) * state[1]
                for m in range(2)
            )
        return state, entering

    def closed(order, pair, first, source):
        start = tuple((row == count + k).astype(f32) for k in range(2))
        (total_one, total_two), _ = through(order, pair, first, source, start)
        a = 1.0 - total_one[count : count + 1]
        b = total_one[count + 1 : count + 2]
        c = total_two[count : count + 1]
        d = 1.0 - total_two[count + 1 : count + 2]
        scale = 1.0 / (a * d - b * c)
        live = row < count
        total_one, total_two = jnp.where(live, total_one, 0.0), jnp.where(live, total_two, 0.0)
        start = ((d * total_one + b * total_two) * scale, (c * total_one + a * total_two) * scale)
        return through(order, pair, first, source, start)[1]

    lower_in = closed(range(blocks), lower, 0, slot)

    def upper_source(p, m):
        z_one, z_two = lower_in[p]
        return slot(p, 2 + m) + entry(upper, p, m, 0) * z_one + entry(upper, p, m, 1) * z_two

    upper_in = closed(list(reversed(range(blocks))), upper, 2, upper_source)
    for i, step in enumerate(targets_of(blocks)):
        for m in range(4):
            picked = jnp.zeros((height, fields), f32)
            for p in range(blocks):
                value = lower_in[p][m] if m < 2 else upper_in[p][m - 2]
                picked = jnp.where(own == (p ^ step), value, picked)
            enter_ref[i, m] = picked[:count]


def rad_table_kernel(coef_ref, own_ref, enter_ref, pivot_ref):
    _, cells, fields = coef_ref.shape
    rows = own_ref.shape[1]
    blocks = cells // rows
    own = lax.axis_index("rad")
    total = 1.0 + coef_ref[0, 0:1]
    for i in range(cells):
        pivot = coef_ref[1, i : i + 1] + total
        pivot_ref[1 + i : 2 + i] = pivot
        if i + 1 < cells:
            total = 1.0 + coef_ref[0, i + 1 : i + 2] * (total / pivot)
    pivot_ref[0:1] = jnp.ones((1, fields), f32)
    lower, upper = coef_ref[0], coef_ref[1]
    first = lax.broadcasted_iota(jnp.int32, (cells, fields), 0) == 0
    scale = jnp.sqrt(jnp.sqrt(1.0 + lower + upper))
    inverse = 1.0 / pivot_ref[1 : cells + 1]
    forward = jnp.where(first, 0.0, lower / pivot_ref[0:cells])
    backward = upper * inverse
    for kind, table in enumerate((scale, forward, inverse, backward)):
        picked = jnp.zeros((rows, fields), f32)
        for p in range(blocks):
            picked = jnp.where(own == p, table[p * rows : (p + 1) * rows], picked)
        own_ref[kind] = picked

    maps = []
    for p in range(blocks):
        lines = [slice(p * rows + i, p * rows + i + 1) for i in range(rows)]
        ahead, held = jnp.ones((1, fields), f32), []
        for line in lines:
            ahead = forward[line] * ahead
            held.append(ahead)
        back, gain = jnp.zeros((1, fields), f32), jnp.ones((1, fields), f32)
        for line, value in zip(reversed(lines), reversed(held)):
            back = inverse[line] * value + backward[line] * back
            gain = backward[line] * gain
        maps.append((ahead, back, gain))
    count = 2 * blocks
    height = -(-count // 8) * 8
    row = lax.broadcasted_iota(jnp.int32, (height, fields), 0)

    def slot(p, k):
        return (row == 2 * (p ^ own) + k).astype(f32)

    zero = jnp.zeros((height, fields), f32)
    ahead, ahead_in = zero, {}
    for p in range(blocks):
        ahead_in[p] = ahead
        ahead = slot(p, 0) + maps[p][0] * ahead
    back, back_in = zero, {}
    for p in reversed(range(blocks)):
        back_in[p] = back
        back = slot(p, 1) + maps[p][1] * ahead_in[p] + maps[p][2] * back
    for i, step in enumerate(targets_of(blocks)):
        for m, entering in enumerate((ahead_in, back_in)):
            picked = zero
            for p in range(blocks):
                picked = jnp.where(own == (p ^ step), entering[p], picked)
            enter_ref[i, m] = picked[:count]


def from_partner(values, axis, step):
    if step == 0:
        return values
    return lax.ppermute(values, axis, [(i, i ^ step) for i in range(lax.axis_size(axis))])


def local(residual, left_vec, dissip, azim_coef, radial_coef):
    fields, cells, rows, width = residual.shape
    azim_count, rad_count = lax.axis_size("azim"), lax.axis_size("rad")
    whole, flat = (fields, cells, rows, width), (fields * cells * rows, width)
    vec = left_vec.reshape(-1)
    azim_blocks = azim_coef.reshape(4, fields, azim_count, cells).transpose(0, 2, 3, 1)
    reply = call(reply_kernel, [(4, cells, fields)], 0, 1)(azim_blocks)[0]
    reply = jnp.pad(reply.transpose(2, 0, 1), ((0, 0), (0, 0), (0, width - cells)))
    weights = jnp.sqrt(1.0 - (azim_coef[0::2] + azim_coef[1::2]) ** 2)
    kinds = jnp.concatenate([azim_coef[:2], weights[:1], azim_coef[2:], weights[1:]])
    own_azim = lax.dynamic_slice_in_dim(kinds, lax.axis_index("azim") * cells, cells, 2).reshape(-1)

    edge = call(edge_kernel, [(fields, rows, width)], 0, 1)(residual)[0]
    halo = from_partner(edge, "axial", 1)

    azim_enter = call(
        azim_table_kernel, [(len(targets_of(azim_count)), 4, 4 * azim_count, fields)], 0, 1
    )(azim_blocks)[0]
    own_rad, rad_enter = call(
        rad_table_kernel,
        [(4, rows, fields), (len(targets_of(rad_count)), 2, 2 * rad_count, fields)],
        0,
        1,
        [(rad_count * rows + 8, fields)],
    )(radial_coef.transpose(0, 2, 1))
    azim_enter, rad_enter = azim_enter.reshape(-1), rad_enter.reshape(-1)
    own_rad = own_rad.transpose(0, 2, 1).reshape(-1)

    src, states = call(first_kernel, [whole, (fields, 4, rows, width)], 3, 1, [whole])(
        own_azim, vec, dissip, residual
    )
    half = (fields, 4, rows // 2, width)
    small = (fields, 8, width)
    one, two, part, end = call(
        patch_kernel, [half, half, (fields, rows, width), small], 3, 3, [(fields * 4 * rows, width)]
    )(vec, dissip, own_rad, halo, states, reply)
    low, high = low_high(azim_count)
    ones = [from_partner(one, "azim", s) for s in low]
    twos = [from_partner(two, "azim", s) for s in high]

    smalls = [from_partner(end, "rad", s) for s in range(rad_count)]
    src, ends = call(source_kernel, [flat, (fields, 2, cells, width)], 1, 2)(own_rad, src, part)

    message = (fields, 5, rows // 2, width)
    *sums, lone = call(
        lambda *refs: send_kernel(azim_count, low, high, rad_count, *refs),
        [message] * (len(low) + len(high)) + [small],
        2,
        len(low) + len(high) + rad_count,
        cost=10**11,
    )(azim_enter, rad_enter, *ones, *twos, *smalls)
    near, far = low_high(rad_count)
    gathered = [from_partner(ends, "rad", s) for s in near]
    entry = call(
        lambda enter_ref, after_ref, *refs: spread_kernel(rad_count, 2, near, far, enter_ref, *refs),
        [ends.shape] * len(far),
        1,
        len(near) + 1,
    )(rad_enter, lone, *gathered)
    entry = [from_partner(value, "rad", s) for s, value in zip(far, entry)]
    src = call(radial_kernel, [flat], 1, len(far) + 1)(own_rad, *entry, src)[0]

    rest = [s for s in range(azim_count) if s not in low + high]
    parts = [from_partner(value, "azim", s) for s, value in zip(high + low, sums)]
    parts += [from_partner(lone, "azim", s) for s in rest]

    chunks = 4
    return pl.pallas_call(
        lambda *refs: last_kernel(len(high), len(low), high + low + rest, *refs),
        out_shape=jax.ShapeDtypeStruct(whole, f32),
        in_specs=[SMEM] * 3 + [VMEM] * (len(parts) + 1),
        out_specs=pl.BlockSpec(memory_space=pl.ANY),
        scratch_shapes=[
            pltpu.VMEM(whole, f32),
            pltpu.VMEM((fields * 4 * rows, width), f32),
            pltpu.VMEM(whole, f32),
            pltpu.SemaphoreType.DMA((chunks,)),
        ],
        compiler_params=params,
    )(own_azim, azim_enter, own_rad, *parts, src.reshape(whole))


def solution(mesh):
    placed = (P(None, "azim", "rad", "axial"), P(), P(), P(), P())
    return jax.shard_map(
        local,
        mesh=mesh,
        in_specs=placed,
        out_specs=P(None, "azim", "rad", "axial"),
        check_vma=False,
    )
```

```python
import jax
import jax.numpy as jnp
from jax import lax
from jax.experimental import pallas as pl
from jax.experimental.pallas import tpu as pltpu
from jax.sharding import PartitionSpec as P

f32 = jnp.float32
VMEM = pl.BlockSpec(memory_space=pltpu.VMEM)
params = pltpu.CompilerParams(vmem_limit_bytes=32 * 1024 * 1024)


def call(body, outs, *operands, scratch=(), cost=0):
    return pl.pallas_call(
        body,
        out_shape=[jax.ShapeDtypeStruct(shape, f32) for shape in outs],
        in_specs=[VMEM] * len(operands),
        out_specs=[VMEM] * len(outs),
        scratch_shapes=[pltpu.VMEM(shape, f32) for shape in scratch],
        compiler_params=params,
        cost_estimate=pl.CostEstimate(flops=cost, bytes_accessed=0, transcendentals=0),
    )(*operands)


def over_lanes(column, width):
    return jnp.broadcast_to(column, (column.shape[0], width))


def lanes_of(shape):
    return lax.broadcasted_iota(jnp.int32, shape, len(shape) - 1)


def low_high(count):
    split = 1 << ((count.bit_length() - 1) // 2)
    return list(range(split)), list(range(0, count, split))


def targets_of(count):
    low, high = low_high(count)
    return low + high[1:]


def far_lane(width):
    return jnp.where(lax.axis_index("axial") == 0, width - 1, 0)


def edge_kernel(res_ref, edge_ref):
    fields, cells, rows, width = res_ref.shape
    source = far_lane(width)
    lane = lanes_of((rows, width))
    packed = [jnp.zeros((rows, width), f32)] * fields
    for j in range(cells):
        for f in range(fields):
            moved = pltpu.roll(res_ref[f, j], (j - source + width) % width, 1)
            packed[f] = jnp.where(lane == j, moved, packed[f])
    for f in range(fields):
        edge_ref[f] = packed[f]


def lower_sweep(coef_ref, cells, load, z_ref, start):
    fields = len(start)

    def step(j, carry):
        source = load(j)
        out = []
        for f in range(fields):
            one, two = carry[f]
            a, b, w = (coef_ref[kind, j, f : f + 1] for kind in range(3))
            z = w * source[f] + b * two + a * one
            z_ref[f, j] = z
            out.append((z, one))
        return tuple(out)

    return lax.fori_loop(0, cells, step, start, unroll=8)


def upper_sweep(coef_ref, cells, z_ref, start, store=None, first=0, count=None):
    fields = len(start)
    count = cells if count is None else count

    def step(i, carry):
        j = first + count - 1 - i
        out = []
        for f in range(fields):
            one, two = carry[f]
            c, e, w = (coef_ref[kind, j, f : f + 1] for kind in range(3, 6))
            v = w * z_ref[f, j] + e * two + c * one
            if store is not None:
                store(f, j, v)
            out.append((v, one))
        return tuple(out)

    return lax.fori_loop(0, count, step, start, unroll=8)


def radial_sweeps(rad_ref, f, load, ahead, back, store):
    rows = rad_ref.shape[2]

    def coef(kind, i):
        return rad_ref[f, kind, i : i + 1]

    held = []
    for i in range(rows):
        ahead = coef(0, i) * load(i) + coef(1, i) * ahead
        held.append(ahead)
    for i in reversed(range(rows)):
        back = coef(2, i) * held[i] + coef(3, i) * back
        store(i, back)


def radial_ends(rad_ref, f, load):
    last = first = None
    for i in range(rad_ref.shape[2]):
        line = load(i)
        to_last = rad_ref[f, 4, i : i + 1] * line
        to_first = rad_ref[f, 5, i : i + 1] * line
        last = to_last if last is None else last + to_last
        first = to_first if first is None else first + to_first
    return last, first


def mix(mix_ref, values):
    fields = len(values)
    return [sum(mix_ref[f, g : g + 1] * values[f] for f in range(fields)) for g in range(fields)]


def first_kernel(coef_ref, mix_ref, res_ref, src_ref, state_ref, z_ref):
    fields, cells, rows, width = res_ref.shape
    lane = lanes_of((rows, width))

    def load(j):
        out = []
        for f, c in enumerate(mix(mix_ref, [res_ref[f, j] for f in range(fields)])):
            beside = jnp.where(lane == 0, 0.0, pltpu.roll(c, 1, 1)) + jnp.where(
                lane == width - 1, 0.0, pltpu.roll(c, width - 1, 1)
            )
            src = mix_ref[fields + 1, f : f + 1] * c + mix_ref[fields, f : f + 1] * beside
            src_ref[f, j] = src
            out.append(src)
        return out

    state_ref[...] = jnp.zeros(state_ref.shape, f32)
    start = tuple((state_ref[f, 0], state_ref[f, 1]) for f in range(fields))
    carry = lower_sweep(coef_ref, cells, load, z_ref, start)
    for f in range(fields):
        state_ref[f, 0], state_ref[f, 1] = carry[f]
    start = tuple((state_ref[f, 2], state_ref[f, 3]) for f in range(fields))
    carry = upper_sweep(coef_ref, cells, z_ref, start)
    for f in range(fields):
        state_ref[f, 2], state_ref[f, 3] = carry[f]


def patch_kernel(
    mix_ref, rad_ref, halo_ref, state_ref, reply_ref, first_ref, second_ref, part_ref, end_ref, work_ref
):
    fields, _, rows, width = state_ref.shape
    lane = lanes_of((rows, width))
    target = far_lane(width)
    for f, h in enumerate(mix(mix_ref, [halo_ref[f] for f in range(fields)])):
        h = mix_ref[fields, f : f + 1] * h
        part_ref[f] = h
        for m in range(4):
            extra = jnp.sum(h * reply_ref[m, f : f + 1], axis=1, keepdims=True)
            tile = state_ref[f, m] + jnp.where(lane == target, extra, 0.0)
            first_ref[f, m] = tile[: rows // 2]
            second_ref[f, m] = tile[rows // 2 :]
            work_ref[pl.ds((f * 4 + m) * rows, rows)] = tile
    for f in range(fields):
        end_ref[f, 0:4], end_ref[f, 4:8] = radial_ends(
            rad_ref, f, lambda i: work_ref[pl.ds(f * 4 * rows + i, 4, stride=rows)]
        )


def source_kernel(rad_ref, src_ref, part_ref, end_ref, turn_ref):
    fields, _, cells, width = end_ref.shape
    rows = part_ref.shape[1]
    lane = lanes_of((cells, width))
    target = far_lane(width)
    turn_ref[...] = jnp.zeros(turn_ref.shape, f32)
    for f in range(fields):
        ends = radial_ends(rad_ref, f, lambda i: part_ref[f, i : i + 1])
        turn_ref[2 * f : 2 * f + 1], turn_ref[2 * f + 1 : 2 * f + 2] = ends
    turned = jnp.transpose(turn_ref[...])[:cells]
    for f in range(fields):
        ends = radial_ends(
            rad_ref, f, lambda i: src_ref[pl.ds(f * cells * rows + i, cells, stride=rows)]
        )
        for k in range(2):
            moved = pltpu.roll(turned, (target - (2 * f + k) + width) % width, 1)
            end_ref[f, k] = ends[k] + jnp.where(lane == target, moved, 0.0)


def weighted(enter_ref, f, target, m, pieces):
    total = None
    for column, value in pieces:
        term = enter_ref[f, target, m, column : column + 1] * value
        total = term if total is None else total + term
    return total


def spread_kernel(count, size, near, far, enter_ref, *refs):
    arrays, sums = refs[: len(near)], refs[len(near) :]
    fields = sums[0].shape[0]
    for s, out_ref in zip(far, sums):
        target = targets_of(count).index(s)
        for f in range(fields):
            pieces = [(size * n + k, ref[f, k]) for n, ref in zip(near, arrays) for k in range(size)]
            for m in range(size):
                out_ref[f, m] = weighted(enter_ref, f, target, m, pieces)


def send_kernel(count, near, far, rads, enter_ref, rad_enter_ref, *refs):
    firsts, refs = refs[: len(near)], refs[len(near) :]
    seconds, refs = refs[: len(far)], refs[len(far) :]
    ends, outs = refs[:rads], refs[rads:]
    fields = ends[0].shape[0]
    spread_kernel(count, 4, near, far, enter_ref, *firsts, *outs[: len(far)])
    spread_kernel(count, 4, far, near, enter_ref, *seconds, *outs[len(far) : -1])
    for f in range(fields):
        pieces = [(2 * s + k, ends[s][f, 4 * k : 4 * k + 4]) for s in range(rads) for k in range(2)]
        for m in range(2):
            own = weighted(rad_enter_ref, f, 0, m, pieces)
            for out_ref in outs[:-1]:
                out_ref[f, 4, 4 * m : 4 * m + 4] = own
            outs[-1][f, 4 * m : 4 * m + 4] = own


def radial_kernel(rad_ref, *refs):
    ends, (src_ref, part_ref, out_ref, all_ref) = refs[:-4], refs[-4:]
    fields, _, cells, width = ends[0].shape
    rows = part_ref.shape[1]
    lane = lanes_of((rows, width))
    target = far_lane(width)
    for f in range(fields):
        for j in range(cells):
            at = pl.ds((f * cells + j) * rows, rows)
            moved = pltpu.roll(part_ref[f], (target - j + width) % width, 1)
            all_ref[at] = src_ref[at] + jnp.where(lane == target, moved, 0.0)
    for f in range(fields):
        for first in range(0, cells, 16):

            def at(i):
                return pl.ds((f * cells + first) * rows + i, 16, stride=rows)

            def store(i, value):
                out_ref[at(i)] = value

            ahead, back = (sum(ref[f, m, first : first + 16] for ref in ends) for m in range(2))
            radial_sweeps(rad_ref, f, lambda i: all_ref[at(i)], ahead, back, store)


def last_kernel(firsts, seconds, steps, coef_ref, enter_ref, rad_ref, *refs):
    parts, (src_ref, out_ref, z_ref, work_ref, held_ref, sems) = refs[:-6], refs[-6:]
    fields, cells, rows, width = src_ref.shape
    half = rows // 2
    at = {s: i for i, s in reversed(list(enumerate(steps)))}
    upper_rows = lax.broadcasted_iota(jnp.int32, (8, width), 0) < 4
    entry = []
    for f in range(fields):
        for m in range(4):
            base = (f * 4 + m) * rows
            work_ref[pl.ds(base, half)] = sum(ref[f, m] for ref in parts[:firsts])
            work_ref[pl.ds(base + half, half)] = sum(ref[f, m] for ref in parts[firsts : firsts + seconds])

        def row(s, k):
            ref = parts[at[s]]
            if at[s] < firsts + seconds:
                return ref[f, 4, k : k + 1]
            return ref[f, k : k + 1]

        sides = None
        for s in range(len(at)):
            for k in range(4):
                value = jnp.where(upper_rows, row(s, k), row(s, 4 + k))
                term = enter_ref[f, 4 * s + k] * value
                sides = term if sides is None else sides + term

        def store(i, value):
            work_ref[pl.ds(f * 4 * rows + i, 4, stride=rows)] = value

        radial_sweeps(
            rad_ref,
            f,
            lambda i: work_ref[pl.ds(f * 4 * rows + i, 4, stride=rows)],
            sides[0:4],
            sides[4:8],
            store,
        )
        entry.append([work_ref[pl.ds((f * 4 + m) * rows, rows)] for m in range(4)])
    lower_sweep(
        coef_ref,
        cells,
        lambda j: [src_ref[f, j] for f in range(fields)],
        z_ref,
        tuple((e[0], e[1]) for e in entry),
    )

    def store(f, j, value):
        held_ref[f, j] = value

    chunks = sems.shape[0]
    size = cells // chunks
    carry = tuple((e[2], e[3]) for e in entry)
    copies = []
    for c in reversed(range(chunks)):
        carry = upper_sweep(coef_ref, cells, z_ref, carry, store, c * size, size)
        copies.append(
            pltpu.make_async_copy(
                held_ref.at[:, pl.ds(c * size, size)], out_ref.at[:, pl.ds(c * size, size)], sems.at[c]
            )
        )
        copies[-1].start()
    for copy in copies:
        copy.wait()


def weight(a, b):
    return jnp.sqrt(1.0 - (a + b) * (a + b))


def own_table_kernel(coef_ref, vec_ref, dis_ref, tab_ref, reply_ref, mix_ref):
    _, cells, fields, width = tab_ref.shape
    total = coef_ref.shape[2]
    start = lax.axis_index("azim") * cells
    a, b, c, e = (pltpu.roll(coef_ref[kind], (total - start) % total, 1)[:, :width] for kind in range(4))
    for kind, table in enumerate((a, b, weight(a, b), c, e, weight(c, e))):
        for j in range(cells):
            tab_ref[kind, j] = over_lanes(table[:, j : j + 1], width)
    lane = lanes_of((fields, width))
    one = two = jnp.zeros((fields, width), f32)
    held = []
    for j in range(cells):
        z = jnp.where(lane == j, tab_ref[2, j], 0.0) + tab_ref[0, j] * one + tab_ref[1, j] * two
        held.append(z)
        one, two = z, one
    reply_ref[0], reply_ref[1] = one, two
    one = two = jnp.zeros((fields, width), f32)
    for j in reversed(range(cells)):
        v = tab_ref[5, j] * held[j] + tab_ref[3, j] * one + tab_ref[4, j] * two
        one, two = v, one
    reply_ref[2], reply_ref[3] = one, two
    for f in range(fields):
        mix_ref[f] = over_lanes(vec_ref[:, f : f + 1], width)
    square = (fields, fields)
    diagonal = lanes_of(square) == lax.broadcasted_iota(jnp.int32, square, 0)
    dis = jnp.sum(jnp.where(diagonal, dis_ref[...], 0.0), axis=1, keepdims=True)
    mix_ref[fields] = over_lanes(dis, width)
    mix_ref[fields + 1] = over_lanes(1.0 - 2.0 * dis, width)


def azim_table_kernel(coef_ref, enter_ref, lone_ref):
    _, blocks, cells, fields = coef_ref.shape
    width = enter_ref.shape[-1]
    own = lax.axis_index("azim")
    unit = lax.broadcasted_iota(jnp.int32, (blocks, 8, fields), 1)

    def ones(k):
        return (unit == k).astype(f32)

    one, two = ones(0), ones(1)
    held = []
    for j in range(cells):
        z = coef_ref[0, :, j : j + 1] * one + coef_ref[1, :, j : j + 1] * two
        held.append(z)
        one, two = z, one
    lower = (one, two)
    one, two = ones(2), ones(3)
    for j in reversed(range(cells)):
        c, e = coef_ref[2, :, j : j + 1], coef_ref[3, :, j : j + 1]
        v = weight(c, e) * held[j] + c * one + e * two
        one, two = v, one
    upper = (one, two)

    def entry(pair, p, m, k):
        return pair[m][p, k : k + 1]

    count = 4 * blocks
    height = -(-(count + 2) // 8) * 8
    row = lax.broadcasted_iota(jnp.int32, (height, fields), 0)

    def slot(p, k):
        return (row == 4 * (p ^ own) + k).astype(f32)

    def through(order, pair, first, source, start):
        state, entering = start, {}
        for p in order:
            entering[p] = state
            state = tuple(
                source(p, m) + entry(pair, p, m, first) * state[0] + entry(pair, p, m, first + 1) * state[1]
                for m in range(2)
            )
        return state, entering

    def closed(order, pair, first, source):
        start = tuple((row == count + k).astype(f32) for k in range(2))
        (total_one, total_two), _ = through(order, pair, first, source, start)
        a = 1.0 - total_one[count : count + 1]
        b = total_one[count + 1 : count + 2]
        c = total_two[count : count + 1]
        d = 1.0 - total_two[count + 1 : count + 2]
        scale = 1.0 / (a * d - b * c)
        live = row < count
        total_one, total_two = jnp.where(live, total_one, 0.0), jnp.where(live, total_two, 0.0)
        start = ((d * total_one + b * total_two) * scale, (c * total_one + a * total_two) * scale)
        return through(order, pair, first, source, start)[1]

    lower_in = closed(range(blocks), lower, 0, slot)

    def upper_source(p, m):
        z_one, z_two = lower_in[p]
        return slot(p, 2 + m) + entry(upper, p, m, 0) * z_one + entry(upper, p, m, 1) * z_two

    upper_in = closed(list(reversed(range(blocks))), upper, 2, upper_source)
    for i, step in enumerate(targets_of(blocks)):
        for m in range(4):
            picked = jnp.zeros((height, fields), f32)
            for p in range(blocks):
                value = lower_in[p][m] if m < 2 else upper_in[p][m - 2]
                picked = jnp.where(own == (p ^ step), value, picked)
            for f in range(fields):
                value = over_lanes(picked[:count, f : f + 1], width)
                enter_ref[f, i, m] = value
                if i == 0:
                    for again in range(2):
                        lone_ref[pl.ds(f * count * 8 + 4 * again + m, count, stride=8)] = value


def rad_table_kernel(coef_ref, own_ref, enter_ref, work_ref):
    _, rows, blocks, fields = coef_ref.shape
    width = enter_ref.shape[-1]
    own = lax.axis_index("rad")
    lower, upper = coef_ref[0], coef_ref[1]
    scale = jnp.sqrt(jnp.sqrt(1.0 + lower + upper))
    one = jnp.ones((blocks, fields), f32)
    forward, inverse, backward, outer, sums = [], [], [], [], []
    for i in range(rows):
        if i == 0:
            factor = lower[0]
            reach, total = factor, one
        else:
            factor = lower[i] * inverse[-1]
            reach, total = factor * reach, 1.0 + factor * total
        forward.append(factor)
        inverse.append(1.0 / (upper[i] + reach + total))
        backward.append(upper[i] * inverse[-1])
        outer.append(inverse[-1] * reach)
        sums.append(inverse[-1] * total)
    to_last, to_first = [None] * rows, [None] * rows
    last = inverse[-1]
    for i in reversed(range(rows)):
        to_last[i] = scale[i] * last
        last = last * forward[i]
    gain = one
    gathered = []
    for i in range(rows):
        gathered.append(gain * inverse[i])
        gain = gain * backward[i]
    first = jnp.zeros((blocks, fields), f32)
    for i in reversed(range(rows)):
        first = gathered[i] + (forward[i + 1] * first if i + 1 < rows else 0.0)
        to_first[i] = scale[i] * first
    last_before, last_after, last_sum = outer[-1], backward[-1], sums[-1]
    first_before = first_sum = 0.0
    for i in reversed(range(rows)):
        first_before = outer[i] + backward[i] * first_before
        first_sum = sums[i] + backward[i] * first_sum
    first_after = gain

    tables = ([scale[i] for i in range(rows)], forward, inverse, backward, to_last, to_first)
    step = work_ref.shape[0] // (6 * rows)
    for kind, table in enumerate(tables):
        for i in range(rows):
            work_ref[pl.ds((kind * rows + i) * step, blocks)] = table[i]
    for kind in range(6):
        picked = work_ref[pl.ds(kind * rows * step + own, rows, stride=step)]
        for f in range(fields):
            own_ref[f, kind] = over_lanes(picked[:, f : f + 1], width)

    count = 2 * blocks
    height = -(-count // 8) * 8
    row = lax.broadcasted_iota(jnp.int32, (height, fields), 0)

    def slot(p, k):
        return (row == 2 * (p ^ own) + k).astype(f32)

    def of(table, p):
        return table[p : p + 1]

    known, share, spare = {}, {}, {}
    known[0], share[0] = slot(0, 0), of(last_after, 0)
    spare[0] = of(last_sum, 0) + of(last_before, 0)
    pivots, ready = {}, {}
    for p in range(1, blocks):
        before, after, total = of(first_before, p), of(first_after, p), of(first_sum, p)
        pivots[p] = 1.0 / (after + total + before * spare[p - 1])
        ready[p] = (slot(p, 1) + before * known[p - 1]) * pivots[p]
        known[p] = slot(p, 0) + of(last_before, p) * (known[p - 1] + share[p - 1] * ready[p])
        share[p] = of(last_after, p) + of(last_before, p) * share[p - 1] * after * pivots[p]
        spare[p] = of(last_sum, p) + of(last_before, p) * pivots[p] * (
            (after + before) * spare[p - 1] + total
        )
    zero = jnp.zeros((height, fields), f32)
    above, below = {blocks - 1: zero}, {0: zero}
    for p in reversed(range(1, blocks)):
        value = ready[p] + of(first_after, p) * pivots[p] * above[p]
        above[p - 1] = value
        below[p] = known[p - 1] + share[p - 1] * value
    for i, step in enumerate(targets_of(blocks)):
        for m, entering in enumerate((below, above)):
            picked = zero
            for p in range(blocks):
                picked = jnp.where(own == (p ^ step), entering[p], picked)
            for f in range(fields):
                enter_ref[f, i, m] = over_lanes(picked[:count, f : f + 1], width)


def from_partner(values, axis, step):
    if step == 0:
        return values
    return lax.ppermute(values, axis, [(i, i ^ step) for i in range(lax.axis_size(axis))])


def local(residual, left_vec, dissip, azim_coef, radial_coef):
    fields, cells, rows, width = residual.shape
    azim_count, rad_count = lax.axis_size("azim"), lax.axis_size("rad")
    whole, flat = (fields, cells, rows, width), (fields * cells * rows, width)
    edge = call(edge_kernel, [(fields, rows, width)], residual)[0]
    halo = from_partner(edge, "axial", 1)

    own_azim, reply, mixing = call(
        own_table_kernel,
        [(6, cells, fields, width), (4, fields, width), (fields + 2, fields, width)],
        azim_coef,
        left_vec,
        dissip.reshape(1, fields),
    )
    azim_blocks = azim_coef.reshape(4, fields, azim_count, cells).transpose(0, 2, 3, 1)
    azim_enter, lone_enter = call(
        azim_table_kernel,
        [
            (fields, len(targets_of(azim_count)), 4, 4 * azim_count, width),
            (fields * 4 * azim_count * 8, width),
        ],
        azim_blocks,
    )
    lone_enter = lone_enter.reshape(fields, 4 * azim_count, 8, width)
    rad_blocks = radial_coef.reshape(2, fields, rad_count, rows).transpose(0, 3, 2, 1)
    own_rad, rad_enter = call(
        rad_table_kernel,
        [(fields, 6, rows, width), (fields, len(targets_of(rad_count)), 2, 2 * rad_count, width)],
        rad_blocks,
        scratch=[(6 * rows * -(-rad_count // 8) * 8, fields)],
    )

    src, states = call(
        first_kernel, [whole, (fields, 4, rows, width)], own_azim, mixing, residual, scratch=[whole]
    )
    half, small = (fields, 4, rows // 2, width), (fields, 8, width)
    one, two, part, end = call(
        patch_kernel,
        [half, half, (fields, rows, width), small],
        mixing,
        own_rad,
        halo,
        states,
        reply,
        scratch=[(fields * 4 * rows, width)],
    )
    low, high = low_high(azim_count)
    ones = [from_partner(one, "azim", s) for s in low]
    twos = [from_partner(two, "azim", s) for s in high]
    smalls = [from_partner(end, "rad", s) for s in range(rad_count)]
    src = src.reshape(flat)
    ends = call(source_kernel, [(fields, 2, cells, width)], own_rad, src, part, scratch=[(width, width)])[0]

    message = (fields, 5, rows // 2, width)
    *sums, lone = call(
        lambda *refs: send_kernel(azim_count, low, high, rad_count, *refs),
        [message] * (len(low) + len(high)) + [small],
        azim_enter,
        rad_enter,
        *ones,
        *twos,
        *smalls,
        cost=10**11,
    )
    near, far = low_high(rad_count)
    gathered = [from_partner(ends, "rad", s) for s in near]
    entry = call(
        lambda enter_ref, after_ref, *refs: spread_kernel(rad_count, 2, near, far, enter_ref, *refs),
        [ends.shape] * len(far),
        rad_enter,
        lone,
        *gathered,
    )
    entry = [from_partner(value, "rad", s) for s, value in zip(far, entry)]
    src = call(radial_kernel, [flat], own_rad, *entry, src, part, scratch=[flat])[0]

    rest = [s for s in range(azim_count) if s not in low + high]
    parts = [from_partner(value, "azim", s) for s, value in zip(high + low, sums)]
    parts += [from_partner(lone, "azim", s) for s in rest]

    chunks = 4
    return pl.pallas_call(
        lambda *refs: last_kernel(len(high), len(low), high + low + rest, *refs),
        out_shape=jax.ShapeDtypeStruct(whole, f32),
        in_specs=[VMEM] * (len(parts) + 4),
        out_specs=pl.BlockSpec(memory_space=pl.ANY),
        scratch_shapes=[
            pltpu.VMEM(whole, f32),
            pltpu.VMEM((fields * 4 * rows, width), f32),
            pltpu.VMEM(whole, f32),
            pltpu.SemaphoreType.DMA((chunks,)),
        ],
        compiler_params=params,
    )(own_azim, lone_enter, own_rad, *parts, src.reshape(whole))


def solution(mesh):
    placed = (P(None, "azim", "rad", "axial"), P(), P(), P(), P())
    return jax.shard_map(
        local,
        mesh=mesh,
        in_specs=placed,
        out_specs=P(None, "azim", "rad", "axial"),
        check_vma=False,
    )
```

```python
import jax
import jax.numpy as jnp
from jax import lax
from jax.experimental import pallas as pl
from jax.experimental.pallas import tpu as pltpu
from jax.sharding import PartitionSpec as P

f32 = jnp.float32
VMEM = pl.BlockSpec(memory_space=pltpu.VMEM)
params = pltpu.CompilerParams(vmem_limit_bytes=32 * 1024 * 1024)


def call(body, outs, *operands, scratch=(), cost=0, aliases={}):
    return pl.pallas_call(
        body,
        out_shape=[jax.ShapeDtypeStruct(shape, f32) for shape in outs],
        in_specs=[VMEM] * len(operands),
        out_specs=[VMEM] * len(outs),
        scratch_shapes=[pltpu.VMEM(shape, f32) for shape in scratch],
        compiler_params=params,
        input_output_aliases=aliases,
        cost_estimate=pl.CostEstimate(flops=cost, bytes_accessed=0, transcendentals=0),
    )(*operands)


def over_lanes(column, width):
    return jnp.broadcast_to(column, (column.shape[0], width))


def lanes_of(shape):
    return lax.broadcasted_iota(jnp.int32, shape, len(shape) - 1)


def low_high(count):
    split = 1 << ((count.bit_length() - 1) // 2)
    return list(range(split)), list(range(0, count, split))


def targets_of(count):
    low, high = low_high(count)
    return low + high[1:]


def far_lane(width):
    return jnp.where(lax.axis_index("axial") == 0, width - 1, 0)


def edge_kernel(res_ref, edge_ref):
    fields, cells, rows, width = res_ref.shape
    source = far_lane(width)
    lane = lanes_of((rows, width))
    packed = [jnp.zeros((rows, width), f32)] * fields
    for j in range(cells):
        for f in range(fields):
            moved = pltpu.roll(res_ref[f, j], (j - source + width) % width, 1)
            packed[f] = jnp.where(lane == j, moved, packed[f])
    for f in range(fields):
        edge_ref[f] = packed[f]


def lower_sweep(coef_ref, cells, load, z_ref, start):
    fields = len(start)

    def step(j, carry):
        source = load(j)
        out = []
        for f in range(fields):
            one, two = carry[f]
            a, b, w = (coef_ref[kind, j, f : f + 1] for kind in range(3))
            z = w * source[f] + b * two + a * one
            z_ref[f, j] = z
            out.append((z, one))
        return tuple(out)

    return lax.fori_loop(0, cells, step, start, unroll=8)


def upper_sweep(coef_ref, cells, z_ref, start, store=None, first=0, count=None):
    fields = len(start)
    count = cells if count is None else count

    def step(i, carry):
        j = first + count - 1 - i
        out = []
        for f in range(fields):
            one, two = carry[f]
            c, e, w = (coef_ref[kind, j, f : f + 1] for kind in range(3, 6))
            v = w * z_ref[f, j] + e * two + c * one
            if store is not None:
                store(f, j, v)
            out.append((v, one))
        return tuple(out)

    return lax.fori_loop(0, count, step, start, unroll=8)


def radial_sweeps(rad_ref, f, load, ahead, back, store):
    rows = rad_ref.shape[2]

    def coef(kind, i):
        return rad_ref[f, kind, i : i + 1]

    held = []
    for i in range(rows):
        ahead = coef(0, i) * load(i) + coef(1, i) * ahead
        held.append(ahead)
    for i in reversed(range(rows)):
        back = coef(2, i) * held[i] + coef(3, i) * back
        store(i, back)


def radial_ends(rad_ref, f, load):
    last = first = None
    for i in range(rad_ref.shape[2]):
        line = load(i)
        to_last = rad_ref[f, 4, i : i + 1] * line
        to_first = rad_ref[f, 5, i : i + 1] * line
        last = to_last if last is None else last + to_last
        first = to_first if first is None else first + to_first
    return last, first


def mix(mix_ref, values):
    fields = len(values)
    return [sum(mix_ref[f, g : g + 1] * values[f] for f in range(fields)) for g in range(fields)]


def first_kernel(coef_ref, mix_ref, res_ref, src_ref, state_ref, z_ref):
    fields, cells, rows, width = res_ref.shape
    lane = lanes_of((rows, width))

    def load(j):
        out = []
        for f, c in enumerate(mix(mix_ref, [res_ref[f, j] for f in range(fields)])):
            beside = jnp.where(lane == 0, 0.0, pltpu.roll(c, 1, 1)) + jnp.where(
                lane == width - 1, 0.0, pltpu.roll(c, width - 1, 1)
            )
            src = mix_ref[fields + 1, f : f + 1] * c + mix_ref[fields, f : f + 1] * beside
            src_ref[f, j] = src
            out.append(src)
        return out

    state_ref[...] = jnp.zeros(state_ref.shape, f32)
    start = tuple((state_ref[f, 0], state_ref[f, 1]) for f in range(fields))
    carry = lower_sweep(coef_ref, cells, load, z_ref, start)
    for f in range(fields):
        state_ref[f, 0], state_ref[f, 1] = carry[f]
    start = tuple((state_ref[f, 2], state_ref[f, 3]) for f in range(fields))
    carry = upper_sweep(coef_ref, cells, z_ref, start)
    for f in range(fields):
        state_ref[f, 2], state_ref[f, 3] = carry[f]


def patch_kernel(
    mix_ref, rad_ref, halo_ref, state_ref, reply_ref, _, first_ref, second_ref, part_ref, end_ref, work_ref
):
    fields, _, rows, width = state_ref.shape
    lane = lanes_of((rows, width))
    target = far_lane(width)
    for f, h in enumerate(mix(mix_ref, [halo_ref[f] for f in range(fields)])):
        h = mix_ref[fields, f : f + 1] * h
        part_ref[f] = h
        for m in range(4):
            extra = jnp.sum(h * reply_ref[m, f : f + 1], axis=1, keepdims=True)
            tile = state_ref[f, m] + jnp.where(lane == target, extra, 0.0)
            first_ref[f, m] = tile[: rows // 2]
            second_ref[f, m] = tile[rows // 2 :]
            work_ref[pl.ds((f * 4 + m) * rows, rows)] = tile
    for f in range(fields):
        ends = radial_ends(rad_ref, f, lambda i: work_ref[pl.ds(f * 4 * rows + i, 4, stride=rows)])
        for k in range(2):
            side = slice(4 * k, 4 * k + 4)
            first_ref[f, 4, side] = second_ref[f, 4, side] = end_ref[f, side] = ends[k]


def source_ends(rad_ref, src_ref, end_ref):
    fields, _, cells, _ = end_ref.shape
    rows = rad_ref.shape[2]
    for f in range(fields):
        end_ref[f, 0], end_ref[f, 1] = radial_ends(
            rad_ref, f, lambda i: src_ref[pl.ds(f * cells * rows + i, cells, stride=rows)]
        )


def halo_ends_kernel(rad_ref, part_ref, known_ref, *refs):
    outs, turn_ref = refs[:-1], refs[-1]
    fields, _, cells, width = known_ref.shape
    lane = lanes_of((cells, width))
    target = far_lane(width)
    size = cells // len(outs)
    turn_ref[...] = jnp.zeros(turn_ref.shape, f32)
    for f in range(fields):
        ends = radial_ends(rad_ref, f, lambda i: part_ref[f, i : i + 1])
        turn_ref[2 * f : 2 * f + 1], turn_ref[2 * f + 1 : 2 * f + 2] = ends
    turned = jnp.transpose(turn_ref[...])[:cells]
    for f in range(fields):
        for k in range(2):
            moved = pltpu.roll(turned, (target - (2 * f + k) + width) % width, 1)
            value = known_ref[f, k] + jnp.where(lane == target, moved, 0.0)
            for i, out_ref in enumerate(outs):
                out_ref[f, k] = value[i * size : (i + 1) * size]


def first_half():
    return lax.axis_index("azim") < lax.axis_size("azim") // 2


def early_kernel(coef_ref, rad_ref, src_ref, enter_ref, lone_ref, end_ref):
    @pl.when(first_half())
    def _():
        azim_table(coef_ref, enter_ref, lone_ref)
        source_ends(rad_ref, src_ref, end_ref)


def late_kernel(coef_ref, rad_ref, src_ref, _, __, ___, enter_ref, lone_ref, end_ref):
    @pl.when(jnp.logical_not(first_half()))
    def _():
        azim_table(coef_ref, enter_ref, lone_ref)
        source_ends(rad_ref, src_ref, end_ref)


def weighted(enter_ref, f, target, m, pieces):
    total = None
    for column, value in pieces:
        term = enter_ref[f, target, m, column : column + 1] * value
        total = term if total is None else total + term
    return total


def spread_kernel(count, size, near, far, enter_ref, *refs):
    arrays, sums = refs[: -len(far)], refs[-len(far) :]
    parts = len(arrays) // len(near)
    extent = arrays[0].shape[2]
    for s, out_ref in zip(far, sums):
        target = targets_of(count).index(s)
        for part in range(parts):
            for f in range(out_ref.shape[0]):
                pieces = [
                    (size * n + k, ref[f, k]) for n, ref in zip(near, arrays[part::parts]) for k in range(size)
                ]
                for m in range(size):
                    value = weighted(enter_ref, f, target, m, pieces)
                    out_ref[f, m, part * extent : (part + 1) * extent] = value


def send_kernel(count, near, far, enter_ref, *refs):
    firsts, refs = refs[: len(near)], refs[len(near) :]
    seconds, refs = refs[: len(far)], refs[len(far) :]
    spread_kernel(count, 4, near, far, enter_ref, *firsts, *refs[: len(far)])
    spread_kernel(count, 4, far, near, enter_ref, *seconds, *refs[len(far) :])


def pass_kernel(in_ref, out_ref):
    out_ref[...] = in_ref[...]


def entry_end_kernel(steps, enter_ref, *refs):
    parts, out_ref = refs[:-1], refs[-1]
    fields, _, width = out_ref.shape
    upper_rows = lax.broadcasted_iota(jnp.int32, (8, width), 0) < 4
    for f in range(fields):
        total = None
        for s, ref in zip(steps, parts):
            for k in range(4):
                here = ref.at[f, 4] if len(ref.shape) == 4 else ref.at[f]
                value = jnp.where(upper_rows, here[k : k + 1], here[4 + k : 5 + k])
                term = enter_ref[f, 4 * s + k] * value
                total = term if total is None else total + term
        out_ref[f] = total


def radial_kernel(rad_ref, *refs):
    ends, (src_ref, part_ref, out_ref, all_ref) = refs[:-4], refs[-4:]
    fields, rows, width = part_ref.shape
    cells = src_ref.shape[0] // (fields * rows)
    lane = lanes_of((rows, width))
    target = far_lane(width)
    for f in range(fields):
        for j in range(cells):
            at = pl.ds((f * cells + j) * rows, rows)
            moved = pltpu.roll(part_ref[f], (target - j + width) % width, 1)
            all_ref[at] = src_ref[at] + jnp.where(lane == target, moved, 0.0)
    for f in range(fields):
        for first in range(0, cells, 16):

            def at(i):
                return pl.ds((f * cells + first) * rows + i, 16, stride=rows)

            def store(i, value):
                out_ref[at(i)] = value

            ahead, back = (sum(ref[f, m, first : first + 16] for ref in ends) for m in range(2))
            radial_sweeps(rad_ref, f, lambda i: all_ref[at(i)], ahead, back, store)


def last_kernel(firsts, seconds, coef_ref, rad_enter_ref, rad_ref, *refs):
    parts, (src_ref, out_ref, z_ref, work_ref, held_ref, sems) = refs[:-6], refs[-6:]
    fields, cells, rows, width = src_ref.shape
    half = rows // 2
    ends = parts[firsts + seconds :]
    entry = []
    for f in range(fields):
        for m in range(4):
            base = (f * 4 + m) * rows
            work_ref[pl.ds(base, half)] = sum(ref[f, m] for ref in parts[:firsts])
            work_ref[pl.ds(base + half, half)] = sum(ref[f, m] for ref in parts[firsts : firsts + seconds])
        pieces = [(2 * s + k, ref[f, 4 * k : 4 * k + 4]) for s, ref in enumerate(ends) for k in range(2)]

        def store(i, value):
            work_ref[pl.ds(f * 4 * rows + i, 4, stride=rows)] = value

        radial_sweeps(
            rad_ref,
            f,
            lambda i: work_ref[pl.ds(f * 4 * rows + i, 4, stride=rows)],
            *(weighted(rad_enter_ref, f, 0, m, pieces) for m in range(2)),
            store,
        )
        entry.append([work_ref[pl.ds((f * 4 + m) * rows, rows)] for m in range(4)])
    lower_sweep(
        coef_ref,
        cells,
        lambda j: [src_ref[f, j] for f in range(fields)],
        z_ref,
        tuple((e[0], e[1]) for e in entry),
    )

    def store(f, j, value):
        held_ref[f, j] = value

    chunks = sems.shape[0]
    size = cells // chunks
    carry = tuple((e[2], e[3]) for e in entry)
    copies = []
    for c in reversed(range(chunks)):
        carry = upper_sweep(coef_ref, cells, z_ref, carry, store, c * size, size)
        copies.append(
            pltpu.make_async_copy(
                held_ref.at[:, pl.ds(c * size, size)], out_ref.at[:, pl.ds(c * size, size)], sems.at[c]
            )
        )
        copies[-1].start()
    for copy in copies:
        copy.wait()


def weight(a, b):
    return jnp.sqrt(1.0 - (a + b) * (a + b))


def own_table_kernel(coef_ref, vec_ref, dis_ref, tab_ref, reply_ref, mix_ref):
    _, cells, fields, width = tab_ref.shape
    total = coef_ref.shape[2]
    start = lax.axis_index("azim") * cells
    a, b, c, e = (pltpu.roll(coef_ref[kind], (total - start) % total, 1)[:, :width] for kind in range(4))
    for kind, table in enumerate((a, b, weight(a, b), c, e, weight(c, e))):
        for j in range(cells):
            tab_ref[kind, j] = over_lanes(table[:, j : j + 1], width)
    lane = lanes_of((fields, width))
    one = two = jnp.zeros((fields, width), f32)
    held = []
    for j in range(cells):
        z = jnp.where(lane == j, tab_ref[2, j], 0.0) + tab_ref[0, j] * one + tab_ref[1, j] * two
        held.append(z)
        one, two = z, one
    reply_ref[0], reply_ref[1] = one, two
    one = two = jnp.zeros((fields, width), f32)
    for j in reversed(range(cells)):
        v = tab_ref[5, j] * held[j] + tab_ref[3, j] * one + tab_ref[4, j] * two
        one, two = v, one
    reply_ref[2], reply_ref[3] = one, two
    for f in range(fields):
        mix_ref[f] = over_lanes(vec_ref[:, f : f + 1], width)
    square = (fields, fields)
    diagonal = lanes_of(square) == lax.broadcasted_iota(jnp.int32, square, 0)
    dis = jnp.sum(jnp.where(diagonal, dis_ref[...], 0.0), axis=1, keepdims=True)
    mix_ref[fields] = over_lanes(dis, width)
    mix_ref[fields + 1] = over_lanes(1.0 - 2.0 * dis, width)


def azim_table(coef_ref, enter_ref, lone_ref):
    _, blocks, cells, fields = coef_ref.shape
    width = enter_ref.shape[-1]
    own = lax.axis_index("azim")
    unit = lax.broadcasted_iota(jnp.int32, (blocks, 8, fields), 1)

    def ones(k):
        return (unit == k).astype(f32)

    one, two = ones(0), ones(1)
    held = []
    for j in range(cells):
        z = coef_ref[0, :, j : j + 1] * one + coef_ref[1, :, j : j + 1] * two
        held.append(z)
        one, two = z, one
    lower = (one, two)
    one, two = ones(2), ones(3)
    for j in reversed(range(cells)):
        c, e = coef_ref[2, :, j : j + 1], coef_ref[3, :, j : j + 1]
        v = weight(c, e) * held[j] + c * one + e * two
        one, two = v, one
    upper = (one, two)

    def entry(pair, p, m, k):
        return pair[m][p, k : k + 1]

    count = 4 * blocks
    height = -(-(count + 2) // 8) * 8
    row = lax.broadcasted_iota(jnp.int32, (height, fields), 0)

    def slot(p, k):
        return (row == 4 * (p ^ own) + k).astype(f32)

    def through(order, pair, first, source, start):
        state, entering = start, {}
        for p in order:
            entering[p] = state
            state = tuple(
                source(p, m) + entry(pair, p, m, first) * state[0] + entry(pair, p, m, first + 1) * state[1]
                for m in range(2)
            )
        return state, entering

    def closed(order, pair, first, source):
        start = tuple((row == count + k).astype(f32) for k in range(2))
        (total_one, total_two), _ = through(order, pair, first, source, start)
        a = 1.0 - total_one[count : count + 1]
        b = total_one[count + 1 : count + 2]
        c = total_two[count : count + 1]
        d = 1.0 - total_two[count + 1 : count + 2]
        scale = 1.0 / (a * d - b * c)
        live = row < count
        total_one, total_two = jnp.where(live, total_one, 0.0), jnp.where(live, total_two, 0.0)
        start = ((d * total_one + b * total_two) * scale, (c * total_one + a * total_two) * scale)
        return through(order, pair, first, source, start)[1]

    lower_in = closed(range(blocks), lower, 0, slot)

    def upper_source(p, m):
        z_one, z_two = lower_in[p]
        return slot(p, 2 + m) + entry(upper, p, m, 0) * z_one + entry(upper, p, m, 1) * z_two

    upper_in = closed(list(reversed(range(blocks))), upper, 2, upper_source)
    for i, step in enumerate(targets_of(blocks)):
        for m in range(4):
            picked = jnp.zeros((height, fields), f32)
            for p in range(blocks):
                value = lower_in[p][m] if m < 2 else upper_in[p][m - 2]
                picked = jnp.where(own == (p ^ step), value, picked)
            for f in range(fields):
                value = over_lanes(picked[:count, f : f + 1], width)
                enter_ref[f, i, m] = value
                if i == 0:
                    for again in range(2):
                        lone_ref[pl.ds(f * count * 8 + 4 * again + m, count, stride=8)] = value


def rad_table_kernel(coef_ref, own_ref, enter_ref, work_ref):
    _, rows, blocks, fields = coef_ref.shape
    width = enter_ref.shape[-1]
    own = lax.axis_index("rad")
    lower, upper = coef_ref[0], coef_ref[1]
    scale = jnp.sqrt(jnp.sqrt(1.0 + lower + upper))
    one = jnp.ones((blocks, fields), f32)
    forward, inverse, backward, outer, sums = [], [], [], [], []
    for i in range(rows):
        if i == 0:
            factor = lower[0]
            reach, total = factor, one
        else:
            factor = lower[i] * inverse[-1]
            reach, total = factor * reach, 1.0 + factor * total
        forward.append(factor)
        inverse.append(1.0 / (upper[i] + reach + total))
        backward.append(upper[i] * inverse[-1])
        outer.append(inverse[-1] * reach)
        sums.append(inverse[-1] * total)
    to_last, to_first = [None] * rows, [None] * rows
    last = inverse[-1]
    for i in reversed(range(rows)):
        to_last[i] = scale[i] * last
        last = last * forward[i]
    gain = one
    gathered = []
    for i in range(rows):
        gathered.append(gain * inverse[i])
        gain = gain * backward[i]
    first = jnp.zeros((blocks, fields), f32)
    for i in reversed(range(rows)):
        first = gathered[i] + (forward[i + 1] * first if i + 1 < rows else 0.0)
        to_first[i] = scale[i] * first
    last_before, last_after, last_sum = outer[-1], backward[-1], sums[-1]
    first_before = first_sum = 0.0
    for i in reversed(range(rows)):
        first_before = outer[i] + backward[i] * first_before
        first_sum = sums[i] + backward[i] * first_sum
    first_after = gain

    tables = ([scale[i] for i in range(rows)], forward, inverse, backward, to_last, to_first)
    step = work_ref.shape[0] // (6 * rows)
    for kind, table in enumerate(tables):
        for i in range(rows):
            work_ref[pl.ds((kind * rows + i) * step, blocks)] = table[i]
    for kind in range(6):
        picked = work_ref[pl.ds(kind * rows * step + own, rows, stride=step)]
        for f in range(fields):
            own_ref[f, kind] = over_lanes(picked[:, f : f + 1], width)

    count = 2 * blocks
    height = -(-count // 8) * 8
    row = lax.broadcasted_iota(jnp.int32, (height, fields), 0)

    def slot(p, k):
        return (row == 2 * (p ^ own) + k).astype(f32)

    def of(table, p):
        return table[p : p + 1]

    known, share, spare = {}, {}, {}
    known[0], share[0] = slot(0, 0), of(last_after, 0)
    spare[0] = of(last_sum, 0) + of(last_before, 0)
    pivots, ready = {}, {}
    for p in range(1, blocks):
        before, after, total = of(first_before, p), of(first_after, p), of(first_sum, p)
        pivots[p] = 1.0 / (after + total + before * spare[p - 1])
        ready[p] = (slot(p, 1) + before * known[p - 1]) * pivots[p]
        known[p] = slot(p, 0) + of(last_before, p) * (known[p - 1] + share[p - 1] * ready[p])
        share[p] = of(last_after, p) + of(last_before, p) * share[p - 1] * after * pivots[p]
        spare[p] = of(last_sum, p) + of(last_before, p) * pivots[p] * (
            (after + before) * spare[p - 1] + total
        )
    zero = jnp.zeros((height, fields), f32)
    above, below = {blocks - 1: zero}, {0: zero}
    for p in reversed(range(1, blocks)):
        value = ready[p] + of(first_after, p) * pivots[p] * above[p]
        above[p - 1] = value
        below[p] = known[p - 1] + share[p - 1] * value
    for i, step in enumerate(targets_of(blocks)):
        for m, entering in enumerate((below, above)):
            picked = zero
            for p in range(blocks):
                picked = jnp.where(own == (p ^ step), entering[p], picked)
            for f in range(fields):
                enter_ref[f, i, m] = over_lanes(picked[:count, f : f + 1], width)


def from_partner(values, axis, step):
    if step == 0:
        return values
    return lax.ppermute(values, axis, [(i, i ^ step) for i in range(lax.axis_size(axis))])


def local(residual, left_vec, dissip, azim_coef, radial_coef):
    fields, cells, rows, width = residual.shape
    azim_count, rad_count = lax.axis_size("azim"), lax.axis_size("rad")
    whole, flat = (fields, cells, rows, width), (fields * cells * rows, width)
    edge = call(edge_kernel, [(fields, rows, width)], residual)[0]
    halo = from_partner(edge, "axial", 1)

    own_azim, reply, mixing = call(
        own_table_kernel,
        [(6, cells, fields, width), (4, fields, width), (fields + 2, fields, width)],
        azim_coef,
        left_vec,
        dissip.reshape(1, fields),
    )
    azim_blocks = azim_coef.reshape(4, fields, azim_count, cells).transpose(0, 2, 3, 1)
    rad_blocks = radial_coef.reshape(2, fields, rad_count, rows).transpose(0, 3, 2, 1)
    own_rad, rad_enter = call(
        rad_table_kernel,
        [(fields, 6, rows, width), (fields, len(targets_of(rad_count)), 2, 2 * rad_count, width)],
        rad_blocks,
        scratch=[(6 * rows * -(-rad_count // 8) * 8, fields)],
    )

    src, states = call(
        first_kernel, [whole, (fields, 4, rows, width)], own_azim, mixing, residual, scratch=[whole]
    )
    src = src.reshape(flat)
    tables = [
        (fields, len(targets_of(azim_count)), 4, 4 * azim_count, width),
        (fields * 4 * azim_count * 8, width),
        (fields, 2, cells, width),
    ]
    known = call(early_kernel, tables, azim_blocks, own_rad, src)
    half, small = (fields, 4, rows // 2, width), (fields, 8, width)
    message = (fields, 5, rows // 2, width)
    one, two, part, end = call(
        patch_kernel,
        [message, message, (fields, rows, width), small],
        mixing,
        own_rad,
        halo,
        states,
        reply,
        known[2],
        scratch=[(fields * 4 * rows, width)],
    )
    far, near = low_high(azim_count)
    ones = [from_partner(one, "azim", s) for s in near]
    twos = [from_partner(two, "azim", s) for s in far]
    steps = near + far[1:] + [s for s in range(azim_count) if s not in near + far]
    lone = [from_partner(end, "azim", s) for s in steps[len(near + far) - 1 :]]
    lone = [call(pass_kernel, [small], value, cost=10**11)[0] for value in lone]
    azim_enter, lone_enter, ends = call(
        late_kernel, tables, azim_blocks, own_rad, src, *known, aliases={3: 0, 4: 1, 5: 2}
    )
    lone_enter = lone_enter.reshape(fields, 4 * azim_count, 8, width)
    low, high = low_high(rad_count)
    ends = call(
        halo_ends_kernel, [(fields, 2, cells // 2, width)] * 2, own_rad, part, ends, scratch=[(width, width)]
    )
    ends = call(
        lambda *refs: spread_kernel(rad_count, 2, low, high, *refs),
        [(fields, 2, cells, width)] * len(high),
        rad_enter,
        *(from_partner(value, "rad", s) for s in low for value in ends),
    )
    ends = [from_partner(value, "rad", s) for s, value in zip(high, ends)]

    sums = call(
        lambda enter_ref, _, *refs: send_kernel(azim_count, near, far, enter_ref, *refs),
        [half] * (len(near) + len(far)),
        azim_enter,
        lone[-1],
        *ones,
        *twos,
        cost=10**11,
    )
    parts = [from_partner(value, "azim", s) for s, value in zip(far + near, sums)]
    end = call(
        lambda enter_ref, _, *refs: entry_end_kernel(steps, enter_ref, *refs),
        [small],
        lone_enter,
        sums[0],
        *ones,
        *twos[1:],
        *lone,
    )[0]
    entry_ends = [from_partner(end, "rad", s) for s in range(rad_count)]

    src = call(radial_kernel, [flat], own_rad, *ends, src, part, scratch=[flat])[0]

    chunks = 4
    return pl.pallas_call(
        lambda *refs: last_kernel(len(far), len(near), *refs),
        out_shape=jax.ShapeDtypeStruct(whole, f32),
        in_specs=[VMEM] * (len(parts + entry_ends) + 4),
        out_specs=pl.BlockSpec(memory_space=pl.ANY),
        scratch_shapes=[
            pltpu.VMEM(whole, f32),
            pltpu.VMEM((fields * 4 * rows, width), f32),
            pltpu.VMEM(whole, f32),
            pltpu.SemaphoreType.DMA((chunks,)),
        ],
        compiler_params=params,
    )(own_azim, rad_enter, own_rad, *parts, *entry_ends, src.reshape(whole))


def solution(mesh):
    placed = (P(None, "azim", "rad", "axial"), P(), P(), P(), P())
    return jax.shard_map(
        local,
        mesh=mesh,
        in_specs=placed,
        out_specs=P(None, "azim", "rad", "axial"),
        check_vma=False,
    )
```

```python
import jax
import jax.numpy as jnp
from jax import lax
from jax.experimental import pallas as pl
from jax.experimental.pallas import tpu as pltpu
from jax.sharding import PartitionSpec as P

f32 = jnp.float32
VMEM = pl.BlockSpec(memory_space=pltpu.VMEM)
params = pltpu.CompilerParams(vmem_limit_bytes=32 * 1024 * 1024)


def call(body, outs, *operands, scratch=(), cost=0, aliases={}):
    return pl.pallas_call(
        body,
        out_shape=[jax.ShapeDtypeStruct(shape, f32) for shape in outs],
        in_specs=[VMEM] * len(operands),
        out_specs=[VMEM] * len(outs),
        scratch_shapes=[pltpu.VMEM(shape, f32) for shape in scratch],
        compiler_params=params,
        input_output_aliases=aliases,
        cost_estimate=pl.CostEstimate(flops=cost, bytes_accessed=0, transcendentals=0),
    )(*operands)


def over_lanes(column, width):
    return jnp.broadcast_to(column, (column.shape[0], width))


def lanes_of(shape):
    return lax.broadcasted_iota(jnp.int32, shape, len(shape) - 1)


def low_high(count):
    split = 1 << ((count.bit_length() - 1) // 2)
    return list(range(split)), list(range(0, count, split))


def targets_of(count):
    low, high = low_high(count)
    return low + high[1:]


def far_lane(width):
    return jnp.where(lax.axis_index("axial") == 0, width - 1, 0)


def edge_kernel(res_ref, edge_ref):
    fields, cells, rows, width = res_ref.shape
    source = far_lane(width)
    lane = lanes_of((rows, width))
    packed = [jnp.zeros((rows, width), f32)] * fields
    for j in range(cells):
        for f in range(fields):
            moved = pltpu.roll(res_ref[f, j], (j - source + width) % width, 1)
            packed[f] = jnp.where(lane == j, moved, packed[f])
    for f in range(fields):
        edge_ref[f] = packed[f]


def lower_sweep(coef_ref, cells, load, z_ref, start):
    fields = len(start)

    def step(j, carry):
        source = load(j)
        out = []
        for f in range(fields):
            one, two = carry[f]
            a, b, w = (coef_ref[kind, j, f : f + 1] for kind in range(3))
            z = w * source[f] + b * two + a * one
            z_ref[f, j] = z
            out.append((z, one))
        return tuple(out)

    return lax.fori_loop(0, cells, step, start, unroll=8)


def upper_sweep(coef_ref, cells, z_ref, start, store=None, first=0, count=None):
    fields = len(start)
    count = cells if count is None else count

    def step(i, carry):
        j = first + count - 1 - i
        out = []
        for f in range(fields):
            one, two = carry[f]
            c, e, w = (coef_ref[kind, j, f : f + 1] for kind in range(3, 6))
            v = w * z_ref[f, j] + e * two + c * one
            if store is not None:
                store(f, j, v)
            out.append((v, one))
        return tuple(out)

    return lax.fori_loop(0, count, step, start, unroll=8)


def radial_sweeps(rad_ref, f, load, ahead, back, store):
    rows = rad_ref.shape[2]

    def coef(kind, i):
        return rad_ref[f, kind, i : i + 1]

    held = []
    for i in range(rows):
        ahead = coef(0, i) * load(i) + coef(1, i) * ahead
        held.append(ahead)
    for i in reversed(range(rows)):
        back = coef(2, i) * held[i] + coef(3, i) * back
        store(i, back)


def radial_ends(rad_ref, f, load):
    last = first = None
    for i in range(rad_ref.shape[2]):
        line = load(i)
        to_last = rad_ref[f, 4, i : i + 1] * line
        to_first = rad_ref[f, 5, i : i + 1] * line
        last = to_last if last is None else last + to_last
        first = to_first if first is None else first + to_first
    return last, first


def mix(mix_ref, values):
    fields = len(values)
    return [sum(mix_ref[f, g : g + 1] * values[f] for f in range(fields)) for g in range(fields)]


def first_kernel(coef_ref, mix_ref, res_ref, src_ref, state_ref, z_ref):
    fields, cells, rows, width = res_ref.shape
    lane = lanes_of((rows, width))

    def load(j):
        out = []
        for f, c in enumerate(mix(mix_ref, [res_ref[f, j] for f in range(fields)])):
            beside = jnp.where(lane == 0, 0.0, pltpu.roll(c, 1, 1)) + jnp.where(
                lane == width - 1, 0.0, pltpu.roll(c, width - 1, 1)
            )
            src = mix_ref[fields + 1, f : f + 1] * c + mix_ref[fields, f : f + 1] * beside
            src_ref[f, j] = src
            out.append(src)
        return out

    state_ref[...] = jnp.zeros(state_ref.shape, f32)
    start = tuple((state_ref[f, 0], state_ref[f, 1]) for f in range(fields))
    carry = lower_sweep(coef_ref, cells, load, z_ref, start)
    for f in range(fields):
        state_ref[f, 0], state_ref[f, 1] = carry[f]
    start = tuple((state_ref[f, 2], state_ref[f, 3]) for f in range(fields))
    carry = upper_sweep(coef_ref, cells, z_ref, start)
    for f in range(fields):
        state_ref[f, 2], state_ref[f, 3] = carry[f]


def patch_kernel(
    mix_ref, rad_ref, halo_ref, state_ref, reply_ref, _, first_ref, second_ref, part_ref, end_ref, work_ref
):
    fields, _, rows, width = state_ref.shape
    lane = lanes_of((rows, width))
    target = far_lane(width)
    for f, h in enumerate(mix(mix_ref, [halo_ref[f] for f in range(fields)])):
        h = mix_ref[fields, f : f + 1] * h
        part_ref[f] = h
        for m in range(4):
            extra = jnp.sum(h * reply_ref[m, f : f + 1], axis=1, keepdims=True)
            tile = state_ref[f, m] + jnp.where(lane == target, extra, 0.0)
            first_ref[f, m] = tile[: rows // 2]
            second_ref[f, m] = tile[rows // 2 :]
            work_ref[pl.ds((f * 4 + m) * rows, rows)] = tile
    for f in range(fields):
        ends = radial_ends(rad_ref, f, lambda i: work_ref[pl.ds(f * 4 * rows + i, 4, stride=rows)])
        for k in range(2):
            side = slice(4 * k, 4 * k + 4)
            first_ref[f, 4, side] = second_ref[f, 4, side] = end_ref[f, side] = ends[k]


def source_ends(rad_ref, src_ref, end_ref):
    fields, _, cells, _ = end_ref.shape
    rows = rad_ref.shape[2]
    for f in range(fields):
        end_ref[f, 0], end_ref[f, 1] = radial_ends(
            rad_ref, f, lambda i: src_ref[pl.ds(f * cells * rows + i, cells, stride=rows)]
        )


def halo_ends_kernel(rad_ref, part_ref, known_ref, *refs):
    outs, turn_ref = refs[:-1], refs[-1]
    fields, _, cells, width = known_ref.shape
    lane = lanes_of((cells, width))
    target = far_lane(width)
    size = cells // len(outs)
    turn_ref[...] = jnp.zeros(turn_ref.shape, f32)
    for f in range(fields):
        ends = radial_ends(rad_ref, f, lambda i: part_ref[f, i : i + 1])
        turn_ref[2 * f : 2 * f + 1], turn_ref[2 * f + 1 : 2 * f + 2] = ends
    turned = jnp.transpose(turn_ref[...])[:cells]
    for f in range(fields):
        for k in range(2):
            moved = pltpu.roll(turned, (target - (2 * f + k) + width) % width, 1)
            value = known_ref[f, k] + jnp.where(lane == target, moved, 0.0)
            for i, out_ref in enumerate(outs):
                out_ref[f, k] = value[i * size : (i + 1) * size]


def first_half():
    return lax.axis_index("azim") < lax.axis_size("azim") // 2


def early_kernel(coef_ref, rad_ref, src_ref, enter_ref, lone_ref, end_ref):
    @pl.when(first_half())
    def _():
        azim_table(coef_ref, enter_ref, lone_ref)
        source_ends(rad_ref, src_ref, end_ref)


def late_kernel(coef_ref, rad_ref, src_ref, _, __, ___, enter_ref, lone_ref, end_ref):
    @pl.when(jnp.logical_not(first_half()))
    def _():
        azim_table(coef_ref, enter_ref, lone_ref)
        source_ends(rad_ref, src_ref, end_ref)


def weighted(enter_ref, f, target, m, pieces):
    total = None
    for column, value in pieces:
        term = enter_ref[f, target, m, column : column + 1] * value
        total = term if total is None else total + term
    return total


def spread_kernel(count, size, near, far, enter_ref, *refs):
    arrays, sums = refs[: -len(far)], refs[-len(far) :]
    parts = len(arrays) // len(near)
    extent = arrays[0].shape[2]
    for s, out_ref in zip(far, sums):
        target = targets_of(count).index(s)
        for part in range(parts):
            for f in range(out_ref.shape[0]):
                pieces = [
                    (size * n + k, ref[f, k]) for n, ref in zip(near, arrays[part::parts]) for k in range(size)
                ]
                for m in range(size):
                    value = weighted(enter_ref, f, target, m, pieces)
                    out_ref[f, m, part * extent : (part + 1) * extent] = value


def send_kernel(count, near, far, enter_ref, *refs):
    firsts, refs = refs[: len(near)], refs[len(near) :]
    seconds, refs = refs[: len(far)], refs[len(far) :]
    spread_kernel(count, 4, near, far, enter_ref, *firsts, *refs[: len(far)])
    spread_kernel(count, 4, far, near, enter_ref, *seconds, *refs[len(far) :])


def pass_kernel(in_ref, out_ref):
    out_ref[...] = in_ref[...]


def entry_end_kernel(steps, enter_ref, *refs):
    parts, out_ref = refs[:-1], refs[-1]
    fields, _, width = out_ref.shape
    upper_rows = lax.broadcasted_iota(jnp.int32, (8, width), 0) < 4
    for f in range(fields):
        total = None
        for s, ref in zip(steps, parts):
            for k in range(4):
                here = ref.at[f, 4] if len(ref.shape) == 4 else ref.at[f]
                value = jnp.where(upper_rows, here[k : k + 1], here[4 + k : 5 + k])
                term = enter_ref[f, 4 * s + k] * value
                total = term if total is None else total + term
        out_ref[f] = total


def radial_kernel(rad_ref, *refs):
    ends, (src_ref, part_ref, out_ref, all_ref) = refs[:-4], refs[-4:]
    fields, rows, width = part_ref.shape
    cells = src_ref.shape[0] // (fields * rows)
    lane = lanes_of((rows, width))
    target = far_lane(width)
    for f in range(fields):
        for j in range(cells):
            at = pl.ds((f * cells + j) * rows, rows)
            moved = pltpu.roll(part_ref[f], (target - j + width) % width, 1)
            all_ref[at] = src_ref[at] + jnp.where(lane == target, moved, 0.0)
    for f in range(fields):
        for first in range(0, cells, 16):

            def at(i):
                return pl.ds((f * cells + first) * rows + i, 16, stride=rows)

            def store(i, value):
                out_ref[at(i)] = value

            ahead, back = (sum(ref[f, m, first : first + 16] for ref in ends) for m in range(2))
            radial_sweeps(rad_ref, f, lambda i: all_ref[at(i)], ahead, back, store)


def last_kernel(firsts, seconds, coef_ref, rad_enter_ref, rad_ref, *refs):
    parts, (src_ref, out_ref, z_ref, work_ref, held_ref, sems) = refs[:-6], refs[-6:]
    fields, cells, rows, width = src_ref.shape
    half = rows // 2
    ends = parts[firsts + seconds :]
    entry = []
    for f in range(fields):
        for m in range(4):
            base = (f * 4 + m) * rows
            work_ref[pl.ds(base, half)] = sum(ref[f, m] for ref in parts[:firsts])
            work_ref[pl.ds(base + half, half)] = sum(ref[f, m] for ref in parts[firsts : firsts + seconds])
        pieces = [(2 * s + k, ref[f, 4 * k : 4 * k + 4]) for s, ref in enumerate(ends) for k in range(2)]

        def store(i, value):
            work_ref[pl.ds(f * 4 * rows + i, 4, stride=rows)] = value

        radial_sweeps(
            rad_ref,
            f,
            lambda i: work_ref[pl.ds(f * 4 * rows + i, 4, stride=rows)],
            *(weighted(rad_enter_ref, f, 0, m, pieces) for m in range(2)),
            store,
        )
        entry.append([work_ref[pl.ds((f * 4 + m) * rows, rows)] for m in range(4)])
    lower_sweep(
        coef_ref,
        cells,
        lambda j: [src_ref[f, j] for f in range(fields)],
        z_ref,
        tuple((e[0], e[1]) for e in entry),
    )

    def store(f, j, value):
        held_ref[f, j] = value

    chunks = sems.shape[0]
    size = cells // chunks
    carry = tuple((e[2], e[3]) for e in entry)
    copies = []
    for c in reversed(range(chunks)):
        carry = upper_sweep(coef_ref, cells, z_ref, carry, store, c * size, size)
        copies.append(
            pltpu.make_async_copy(
                held_ref.at[:, pl.ds(c * size, size)], out_ref.at[:, pl.ds(c * size, size)], sems.at[c]
            )
        )
        copies[-1].start()
    for copy in copies:
        copy.wait()


def weight(a, b):
    return jnp.sqrt(1.0 - (a + b) * (a + b))


def own_table_kernel(coef_ref, vec_ref, dis_ref, tab_ref, reply_ref, mix_ref):
    _, cells, fields, width = tab_ref.shape
    total = coef_ref.shape[2]
    start = lax.axis_index("azim") * cells
    a, b, c, e = (pltpu.roll(coef_ref[kind], (total - start) % total, 1)[:, :width] for kind in range(4))
    for kind, table in enumerate((a, b, weight(a, b), c, e, weight(c, e))):
        for j in range(cells):
            tab_ref[kind, j] = over_lanes(table[:, j : j + 1], width)
    lane = lanes_of((fields, width))
    one = two = jnp.zeros((fields, width), f32)
    held = []
    for j in range(cells):
        z = jnp.where(lane == j, tab_ref[2, j], 0.0) + tab_ref[0, j] * one + tab_ref[1, j] * two
        held.append(z)
        one, two = z, one
    reply_ref[0], reply_ref[1] = one, two
    one = two = jnp.zeros((fields, width), f32)
    for j in reversed(range(cells)):
        v = tab_ref[5, j] * held[j] + tab_ref[3, j] * one + tab_ref[4, j] * two
        one, two = v, one
    reply_ref[2], reply_ref[3] = one, two
    for f in range(fields):
        mix_ref[f] = over_lanes(vec_ref[:, f : f + 1], width)
    square = (fields, fields)
    diagonal = lanes_of(square) == lax.broadcasted_iota(jnp.int32, square, 0)
    dis = jnp.sum(jnp.where(diagonal, dis_ref[...], 0.0), axis=1, keepdims=True)
    mix_ref[fields] = over_lanes(dis, width)
    mix_ref[fields + 1] = over_lanes(1.0 - 2.0 * dis, width)


def azim_table(coef_ref, enter_ref, lone_ref):
    _, blocks, cells, fields = coef_ref.shape
    width = enter_ref.shape[-1]
    own = lax.axis_index("azim")
    unit = lax.broadcasted_iota(jnp.int32, (blocks, 8, fields), 1)

    def ones(k):
        return (unit == k).astype(f32)

    one, two = ones(0), ones(1)
    held = []
    for j in range(cells):
        z = coef_ref[0, :, j : j + 1] * one + coef_ref[1, :, j : j + 1] * two
        held.append(z)
        one, two = z, one
    lower = (one, two)
    one, two = ones(2), ones(3)
    for j in reversed(range(cells)):
        c, e = coef_ref[2, :, j : j + 1], coef_ref[3, :, j : j + 1]
        v = weight(c, e) * held[j] + c * one + e * two
        one, two = v, one
    upper = (one, two)

    def entry(pair, p, m, k):
        return pair[m][p, k : k + 1]

    count = 4 * blocks
    height = -(-(count + 2) // 8) * 8
    row = lax.broadcasted_iota(jnp.int32, (height, fields), 0)

    def slot(p, k):
        return (row == 4 * (p ^ own) + k).astype(f32)

    def through(order, pair, first, source, start):
        state, entering = start, {}
        for p in order:
            entering[p] = state
            state = tuple(
                source(p, m) + entry(pair, p, m, first) * state[0] + entry(pair, p, m, first + 1) * state[1]
                for m in range(2)
            )
        return state, entering

    def closed(order, pair, first, source):
        start = tuple((row == count + k).astype(f32) for k in range(2))
        (total_one, total_two), _ = through(order, pair, first, source, start)
        a = 1.0 - total_one[count : count + 1]
        b = total_one[count + 1 : count + 2]
        c = total_two[count : count + 1]
        d = 1.0 - total_two[count + 1 : count + 2]
        scale = 1.0 / (a * d - b * c)
        live = row < count
        total_one, total_two = jnp.where(live, total_one, 0.0), jnp.where(live, total_two, 0.0)
        start = ((d * total_one + b * total_two) * scale, (c * total_one + a * total_two) * scale)
        return through(order, pair, first, source, start)[1]

    lower_in = closed(range(blocks), lower, 0, slot)

    def upper_source(p, m):
        z_one, z_two = lower_in[p]
        return slot(p, 2 + m) + entry(upper, p, m, 0) * z_one + entry(upper, p, m, 1) * z_two

    upper_in = closed(list(reversed(range(blocks))), upper, 2, upper_source)
    for i, step in enumerate(targets_of(blocks)):
        for m in range(4):
            picked = jnp.zeros((height, fields), f32)
            for p in range(blocks):
                value = lower_in[p][m] if m < 2 else upper_in[p][m - 2]
                picked = jnp.where(own == (p ^ step), value, picked)
            for f in range(fields):
                value = over_lanes(picked[:count, f : f + 1], width)
                enter_ref[f, i, m] = value
                if i == 0:
                    for again in range(2):
                        lone_ref[pl.ds(f * count * 8 + 4 * again + m, count, stride=8)] = value


def rad_table_kernel(coef_ref, own_ref, enter_ref, work_ref):
    _, rows, blocks, fields = coef_ref.shape
    width = enter_ref.shape[-1]
    own = lax.axis_index("rad")
    lower, upper = coef_ref[0], coef_ref[1]
    scale = jnp.sqrt(jnp.sqrt(1.0 + lower + upper))
    one = jnp.ones((blocks, fields), f32)
    forward, inverse, backward, outer, sums = [], [], [], [], []
    for i in range(rows):
        if i == 0:
            factor = lower[0]
            reach, total = factor, one
        else:
            factor = lower[i] * inverse[-1]
            reach, total = factor * reach, 1.0 + factor * total
        forward.append(factor)
        inverse.append(1.0 / (upper[i] + reach + total))
        backward.append(upper[i] * inverse[-1])
        outer.append(inverse[-1] * reach)
        sums.append(inverse[-1] * total)
    to_last, to_first = [None] * rows, [None] * rows
    last = inverse[-1]
    for i in reversed(range(rows)):
        to_last[i] = scale[i] * last
        last = last * forward[i]
    gain = one
    gathered = []
    for i in range(rows):
        gathered.append(gain * inverse[i])
        gain = gain * backward[i]
    first = jnp.zeros((blocks, fields), f32)
    for i in reversed(range(rows)):
        first = gathered[i] + (forward[i + 1] * first if i + 1 < rows else 0.0)
        to_first[i] = scale[i] * first
    last_before, last_after, last_sum = outer[-1], backward[-1], sums[-1]
    first_before = first_sum = 0.0
    for i in reversed(range(rows)):
        first_before = outer[i] + backward[i] * first_before
        first_sum = sums[i] + backward[i] * first_sum
    first_after = gain

    tables = ([scale[i] for i in range(rows)], forward, inverse, backward, to_last, to_first)
    step = work_ref.shape[0] // (6 * rows)
    for kind, table in enumerate(tables):
        for i in range(rows):
            work_ref[pl.ds((kind * rows + i) * step, blocks)] = table[i]
    for kind in range(6):
        picked = work_ref[pl.ds(kind * rows * step + own, rows, stride=step)]
        for f in range(fields):
            own_ref[f, kind] = over_lanes(picked[:, f : f + 1], width)

    count = 2 * blocks
    height = -(-count // 8) * 8
    row = lax.broadcasted_iota(jnp.int32, (height, fields), 0)

    def slot(p, k):
        return (row == 2 * (p ^ own) + k).astype(f32)

    def of(table, p):
        return table[p : p + 1]

    known, share, spare = {}, {}, {}
    known[0], share[0] = slot(0, 0), of(last_after, 0)
    spare[0] = of(last_sum, 0) + of(last_before, 0)
    pivots, ready = {}, {}
    for p in range(1, blocks):
        before, after, total = of(first_before, p), of(first_after, p), of(first_sum, p)
        pivots[p] = 1.0 / (after + total + before * spare[p - 1])
        ready[p] = (slot(p, 1) + before * known[p - 1]) * pivots[p]
        known[p] = slot(p, 0) + of(last_before, p) * (known[p - 1] + share[p - 1] * ready[p])
        share[p] = of(last_after, p) + of(last_before, p) * share[p - 1] * after * pivots[p]
        spare[p] = of(last_sum, p) + of(last_before, p) * pivots[p] * (
            (after + before) * spare[p - 1] + total
        )
    zero = jnp.zeros((height, fields), f32)
    above, below = {blocks - 1: zero}, {0: zero}
    for p in reversed(range(1, blocks)):
        value = ready[p] + of(first_after, p) * pivots[p] * above[p]
        above[p - 1] = value
        below[p] = known[p - 1] + share[p - 1] * value
    for i, step in enumerate(targets_of(blocks)):
        for m, entering in enumerate((below, above)):
            picked = zero
            for p in range(blocks):
                picked = jnp.where(own == (p ^ step), entering[p], picked)
            for f in range(fields):
                enter_ref[f, i, m] = over_lanes(picked[:count, f : f + 1], width)


def from_partner(values, axis, step):
    if step == 0:
        return values
    return lax.ppermute(values, axis, [(i, i ^ step) for i in range(lax.axis_size(axis))])


def local(residual, left_vec, dissip, azim_coef, radial_coef):
    fields, cells, rows, width = residual.shape
    azim_count, rad_count = lax.axis_size("azim"), lax.axis_size("rad")
    whole, flat = (fields, cells, rows, width), (fields * cells * rows, width)
    edge = call(edge_kernel, [(fields, rows, width)], residual)[0]
    halo = from_partner(edge, "axial", 1)

    own_azim, reply, mixing = call(
        own_table_kernel,
        [(6, cells, fields, width), (4, fields, width), (fields + 2, fields, width)],
        azim_coef,
        left_vec,
        dissip.reshape(1, fields),
    )
    azim_blocks = azim_coef.reshape(4, fields, azim_count, cells).transpose(0, 2, 3, 1)
    rad_blocks = radial_coef.reshape(2, fields, rad_count, rows).transpose(0, 3, 2, 1)
    own_rad, rad_enter = call(
        rad_table_kernel,
        [(fields, 6, rows, width), (fields, len(targets_of(rad_count)), 2, 2 * rad_count, width)],
        rad_blocks,
        scratch=[(6 * rows * -(-rad_count // 8) * 8, fields)],
    )

    src, states = call(
        first_kernel, [whole, (fields, 4, rows, width)], own_azim, mixing, residual, scratch=[whole]
    )
    src = src.reshape(flat)
    tables = [
        (fields, len(targets_of(azim_count)), 4, 4 * azim_count, width),
        (fields * 4 * azim_count * 8, width),
        (fields, 2, cells, width),
    ]
    known = call(early_kernel, tables, azim_blocks, own_rad, src)
    half, small = (fields, 4, rows // 2, width), (fields, 8, width)
    message = (fields, 5, rows // 2, width)
    one, two, part, end = call(
        patch_kernel,
        [message, message, (fields, rows, width), small],
        mixing,
        own_rad,
        halo,
        states,
        reply,
        known[2],
        scratch=[(fields * 4 * rows, width)],
    )
    near, far = low_high(azim_count)
    ones = [from_partner(one, "azim", s) for s in near]
    twos = [from_partner(two, "azim", s) for s in far]
    steps = near + far[1:] + [s for s in range(azim_count) if s not in near + far]
    lone = [from_partner(end, "azim", s) for s in steps[len(near + far) - 1 :]]
    lone = [call(pass_kernel, [small], value, cost=6 * 10**8)[0] for value in lone]
    azim_enter, lone_enter, ends = call(
        late_kernel, tables, azim_blocks, own_rad, src, *known, aliases={3: 0, 4: 1, 5: 2}
    )
    lone_enter = lone_enter.reshape(fields, 4 * azim_count, 8, width)
    low, high = low_high(rad_count)
    ends = call(
        halo_ends_kernel, [(fields, 2, cells // 2, width)] * 2, own_rad, part, ends, scratch=[(width, width)]
    )
    ends = call(
        lambda *refs: spread_kernel(rad_count, 2, low, high, *refs),
        [(fields, 2, cells, width)] * len(high),
        rad_enter,
        *(from_partner(value, "rad", s) for s in low for value in ends),
    )
    ends = [from_partner(value, "rad", s) for s, value in zip(high, ends)]

    sums = call(
        lambda *refs: send_kernel(azim_count, near, far, *refs),
        [half] * (len(near) + len(far)),
        azim_enter,
        *ones,
        *twos,
        cost=10**11,
    )
    parts = [from_partner(value, "azim", s) for s, value in zip(far + near, sums)]
    end = call(
        lambda enter_ref, _, *refs: entry_end_kernel(steps, enter_ref, *refs),
        [small],
        lone_enter,
        sums[0],
        *ones,
        *twos[1:],
        *lone,
    )[0]
    entry_ends = [from_partner(end, "rad", s) for s in range(rad_count)]

    src = call(radial_kernel, [flat], own_rad, *ends, src, part, scratch=[flat])[0]

    chunks = 4
    return pl.pallas_call(
        lambda *refs: last_kernel(len(far), len(near), *refs),
        out_shape=jax.ShapeDtypeStruct(whole, f32),
        in_specs=[VMEM] * (len(parts + entry_ends) + 4),
        out_specs=pl.BlockSpec(memory_space=pl.ANY),
        scratch_shapes=[
            pltpu.VMEM(whole, f32),
            pltpu.VMEM((fields * 4 * rows, width), f32),
            pltpu.VMEM(whole, f32),
            pltpu.SemaphoreType.DMA((chunks,)),
        ],
        compiler_params=params,
    )(own_azim, rad_enter, own_rad, *parts, *entry_ends, src.reshape(whole))


def solution(mesh):
    placed = (P(None, "azim", "rad", "axial"), P(), P(), P(), P())
    return jax.shard_map(
        local,
        mesh=mesh,
        in_specs=placed,
        out_specs=P(None, "azim", "rad", "axial"),
        check_vma=False,
    )
```

```python
import jax
import jax.numpy as jnp
from jax import lax
from jax.experimental import pallas as pl
from jax.experimental.pallas import tpu as pltpu
from jax.sharding import PartitionSpec as P

f32 = jnp.float32
VMEM = pl.BlockSpec(memory_space=pltpu.VMEM)
params = pltpu.CompilerParams(vmem_limit_bytes=32 * 1024 * 1024)


def call(body, outs, *operands, scratch=(), cost=0, aliases={}):
    return pl.pallas_call(
        body,
        out_shape=[jax.ShapeDtypeStruct(shape, f32) for shape in outs],
        in_specs=[VMEM] * len(operands),
        out_specs=[VMEM] * len(outs),
        scratch_shapes=[pltpu.VMEM(shape, f32) for shape in scratch],
        compiler_params=params,
        input_output_aliases=aliases,
        cost_estimate=pl.CostEstimate(flops=cost, bytes_accessed=0, transcendentals=0),
    )(*operands)


def over_lanes(column, width):
    return jnp.broadcast_to(column, (column.shape[0], width))


def lanes_of(shape):
    return lax.broadcasted_iota(jnp.int32, shape, len(shape) - 1)


def low_high(count):
    split = 1 << ((count.bit_length() - 1) // 2)
    return list(range(split)), list(range(0, count, split))


def targets_of(count):
    low, high = low_high(count)
    return low + high[1:]


def far_lane(width):
    return jnp.where(lax.axis_index("axial") == 0, width - 1, 0)


def edge_kernel(res_ref, edge_ref):
    fields, cells, rows, width = res_ref.shape
    source = far_lane(width)
    lane = lanes_of((rows, width))
    packed = [jnp.zeros((rows, width), f32)] * fields
    for j in range(cells):
        for f in range(fields):
            moved = pltpu.roll(res_ref[f, j], (j - source + width) % width, 1)
            packed[f] = jnp.where(lane == j, moved, packed[f])
    for f in range(fields):
        edge_ref[f] = packed[f]


def lower_sweep(coef_ref, cells, load, z_ref, start):
    fields = len(start)

    def step(j, carry):
        source = load(j)
        out = []
        for f in range(fields):
            one, two = carry[f]
            a, b, w = (coef_ref[kind, j, f : f + 1] for kind in range(3))
            z = w * source[f] + b * two + a * one
            z_ref[f, j] = z
            out.append((z, one))
        return tuple(out)

    return lax.fori_loop(0, cells, step, start, unroll=8)


def upper_sweep(coef_ref, cells, z_ref, start, store=None, first=0, count=None):
    fields = len(start)
    count = cells if count is None else count

    def step(i, carry):
        j = first + count - 1 - i
        out = []
        for f in range(fields):
            one, two = carry[f]
            c, e, w = (coef_ref[kind, j, f : f + 1] for kind in range(3, 6))
            v = w * z_ref[f, j] + e * two + c * one
            if store is not None:
                store(f, j, v)
            out.append((v, one))
        return tuple(out)

    return lax.fori_loop(0, count, step, start, unroll=8)


def radial_sweeps(rad_ref, f, load, ahead, back, store):
    rows = rad_ref.shape[2]

    def coef(kind, i):
        return rad_ref[f, kind, i : i + 1]

    held = []
    for i in range(rows):
        ahead = coef(0, i) * load(i) + coef(1, i) * ahead
        held.append(ahead)
    for i in reversed(range(rows)):
        back = coef(2, i) * held[i] + coef(3, i) * back
        store(i, back)


def radial_ends(rad_ref, f, load):
    last = first = None
    for i in range(rad_ref.shape[2]):
        line = load(i)
        to_last = rad_ref[f, 4, i : i + 1] * line
        to_first = rad_ref[f, 5, i : i + 1] * line
        last = to_last if last is None else last + to_last
        first = to_first if first is None else first + to_first
    return last, first


def mix(mix_ref, values):
    fields = len(values)
    return [sum(mix_ref[f, g : g + 1] * values[f] for f in range(fields)) for g in range(fields)]


def first_kernel(coef_ref, mix_ref, res_ref, src_ref, state_ref, z_ref):
    fields, cells, rows, width = res_ref.shape
    lane = lanes_of((rows, width))

    def load(j):
        out = []
        for f, c in enumerate(mix(mix_ref, [res_ref[f, j] for f in range(fields)])):
            beside = jnp.where(lane == 0, 0.0, pltpu.roll(c, 1, 1)) + jnp.where(
                lane == width - 1, 0.0, pltpu.roll(c, width - 1, 1)
            )
            src = mix_ref[fields + 1, f : f + 1] * c + mix_ref[fields, f : f + 1] * beside
            src_ref[f, j] = src
            out.append(src)
        return out

    state_ref[...] = jnp.zeros(state_ref.shape, f32)
    start = tuple((state_ref[f, 0], state_ref[f, 1]) for f in range(fields))
    carry = lower_sweep(coef_ref, cells, load, z_ref, start)
    for f in range(fields):
        state_ref[f, 0], state_ref[f, 1] = carry[f]
    start = tuple((state_ref[f, 2], state_ref[f, 3]) for f in range(fields))
    carry = upper_sweep(coef_ref, cells, z_ref, start)
    for f in range(fields):
        state_ref[f, 2], state_ref[f, 3] = carry[f]


def patch_kernel(
    mix_ref, rad_ref, halo_ref, state_ref, reply_ref, _, first_ref, second_ref, part_ref, end_ref, work_ref
):
    fields, _, rows, width = state_ref.shape
    lane = lanes_of((rows, width))
    target = far_lane(width)
    for f, h in enumerate(mix(mix_ref, [halo_ref[f] for f in range(fields)])):
        h = mix_ref[fields, f : f + 1] * h
        part_ref[f] = h
        for m in range(4):
            extra = jnp.sum(h * reply_ref[m, f : f + 1], axis=1, keepdims=True)
            tile = state_ref[f, m] + jnp.where(lane == target, extra, 0.0)
            first_ref[f, m] = tile[: rows // 2]
            second_ref[f, m] = tile[rows // 2 :]
            work_ref[pl.ds((f * 4 + m) * rows, rows)] = tile
    for f in range(fields):
        ends = radial_ends(rad_ref, f, lambda i: work_ref[pl.ds(f * 4 * rows + i, 4, stride=rows)])
        for k in range(2):
            side = slice(4 * k, 4 * k + 4)
            first_ref[f, 4, side] = second_ref[f, 4, side] = end_ref[f, side] = ends[k]


def source_ends(rad_ref, src_ref, end_ref):
    fields, _, cells, _ = end_ref.shape
    rows = rad_ref.shape[2]
    for f in range(fields):
        end_ref[f, 0], end_ref[f, 1] = radial_ends(
            rad_ref, f, lambda i: src_ref[pl.ds(f * cells * rows + i, cells, stride=rows)]
        )


def halo_ends_kernel(rad_ref, part_ref, known_ref, *refs):
    outs, turn_ref = refs[:-1], refs[-1]
    fields, _, cells, width = known_ref.shape
    lane = lanes_of((cells, width))
    target = far_lane(width)
    size = cells // len(outs)
    turn_ref[...] = jnp.zeros(turn_ref.shape, f32)
    for f in range(fields):
        ends = radial_ends(rad_ref, f, lambda i: part_ref[f, i : i + 1])
        turn_ref[2 * f : 2 * f + 1], turn_ref[2 * f + 1 : 2 * f + 2] = ends
    turned = jnp.transpose(turn_ref[...])[:cells]
    for f in range(fields):
        for k in range(2):
            moved = pltpu.roll(turned, (target - (2 * f + k) + width) % width, 1)
            value = known_ref[f, k] + jnp.where(lane == target, moved, 0.0)
            for i, out_ref in enumerate(outs):
                out_ref[f, k] = value[i * size : (i + 1) * size]


def first_half():
    return lax.axis_index("azim") < lax.axis_size("azim") // 4


def azim_blocks(coef_ref, turn_ref, block_ref):
    kinds, blocks, cells, width = block_ref.shape
    fields = coef_ref.shape[1]
    turn_ref[...] = jnp.zeros(turn_ref.shape, f32)
    for kind in range(kinds):
        turn_ref[8 * kind : 8 * kind + fields] = coef_ref[kind]
    turned = jnp.transpose(turn_ref[...])
    for kind in range(kinds):
        block_ref[kind] = pltpu.roll(turned, (width - 8 * kind) % width, 1).reshape(blocks, cells, width)


def early_kernel(coef_ref, rad_ref, src_ref, enter_ref, lone_ref, end_ref, turn_ref, block_ref):
    @pl.when(first_half())
    def _():
        azim_blocks(coef_ref, turn_ref, block_ref)
        azim_table(block_ref, enter_ref, lone_ref)
        source_ends(rad_ref, src_ref, end_ref)


def late_kernel(coef_ref, rad_ref, src_ref, _, __, ___, enter_ref, lone_ref, end_ref, turn_ref, block_ref):
    @pl.when(jnp.logical_not(first_half()))
    def _():
        azim_blocks(coef_ref, turn_ref, block_ref)
        azim_table(block_ref, enter_ref, lone_ref)
        source_ends(rad_ref, src_ref, end_ref)


def weighted(enter_ref, f, target, m, pieces):
    total = None
    for column, value in pieces:
        term = enter_ref[f, target, m, column : column + 1] * value
        total = term if total is None else total + term
    return total


def spread_kernel(count, size, near, far, enter_ref, *refs):
    arrays, sums = refs[: -len(far)], refs[-len(far) :]
    parts = len(arrays) // len(near)
    extent = arrays[0].shape[2]
    for s, out_ref in zip(far, sums):
        target = targets_of(count).index(s)
        for part in range(parts):
            for f in range(out_ref.shape[0]):
                pieces = [
                    (size * n + k, ref[f, k]) for n, ref in zip(near, arrays[part::parts]) for k in range(size)
                ]
                for m in range(size):
                    value = weighted(enter_ref, f, target, m, pieces)
                    out_ref[f, m, part * extent : (part + 1) * extent] = value


def send_kernel(count, near, far, enter_ref, *refs):
    firsts, refs = refs[: len(near)], refs[len(near) :]
    seconds, refs = refs[: len(far)], refs[len(far) :]
    spread_kernel(count, 4, near, far, enter_ref, *firsts, *refs[: len(far)])
    spread_kernel(count, 4, far, near, enter_ref, *seconds, *refs[len(far) :])


def pass_kernel(in_ref, out_ref):
    out_ref[...] = in_ref[...]


def entry_end_kernel(steps, enter_ref, *refs):
    parts, out_ref = refs[:-1], refs[-1]
    fields, _, width = out_ref.shape
    upper_rows = lax.broadcasted_iota(jnp.int32, (8, width), 0) < 4
    for f in range(fields):
        total = None
        for s, ref in zip(steps, parts):
            for k in range(4):
                here = ref.at[f, 4] if len(ref.shape) == 4 else ref.at[f]
                value = jnp.where(upper_rows, here[k : k + 1], here[4 + k : 5 + k])
                term = enter_ref[f, 4 * s + k] * value
                total = term if total is None else total + term
        out_ref[f] = total


def radial_kernel(rad_ref, *refs):
    ends, (src_ref, part_ref, out_ref, all_ref) = refs[:-4], refs[-4:]
    fields, rows, width = part_ref.shape
    cells = src_ref.shape[0] // (fields * rows)
    lane = lanes_of((rows, width))
    target = far_lane(width)
    for f in range(fields):
        for j in range(cells):
            at = pl.ds((f * cells + j) * rows, rows)
            moved = pltpu.roll(part_ref[f], (target - j + width) % width, 1)
            all_ref[at] = src_ref[at] + jnp.where(lane == target, moved, 0.0)
    for f in range(fields):
        for first in range(0, cells, 16):

            def at(i):
                return pl.ds((f * cells + first) * rows + i, 16, stride=rows)

            def store(i, value):
                out_ref[at(i)] = value

            ahead, back = (sum(ref[f, m, first : first + 16] for ref in ends) for m in range(2))
            radial_sweeps(rad_ref, f, lambda i: all_ref[at(i)], ahead, back, store)


def last_kernel(firsts, seconds, coef_ref, rad_enter_ref, rad_ref, *refs):
    parts, (src_ref, out_ref, z_ref, work_ref, held_ref, sems) = refs[:-6], refs[-6:]
    fields, cells, rows, width = src_ref.shape
    half = rows // 2
    ends = parts[firsts + seconds :]
    entry = []
    for f in range(fields):
        for m in range(4):
            base = (f * 4 + m) * rows
            work_ref[pl.ds(base, half)] = sum(ref[f, m] for ref in parts[:firsts])
            work_ref[pl.ds(base + half, half)] = sum(ref[f, m] for ref in parts[firsts : firsts + seconds])
        pieces = [(2 * s + k, ref[f, 4 * k : 4 * k + 4]) for s, ref in enumerate(ends) for k in range(2)]

        def store(i, value):
            work_ref[pl.ds(f * 4 * rows + i, 4, stride=rows)] = value

        radial_sweeps(
            rad_ref,
            f,
            lambda i: work_ref[pl.ds(f * 4 * rows + i, 4, stride=rows)],
            *(weighted(rad_enter_ref, f, 0, m, pieces) for m in range(2)),
            store,
        )
        entry.append([work_ref[pl.ds((f * 4 + m) * rows, rows)] for m in range(4)])
    lower_sweep(
        coef_ref,
        cells,
        lambda j: [src_ref[f, j] for f in range(fields)],
        z_ref,
        tuple((e[0], e[1]) for e in entry),
    )

    def store(f, j, value):
        held_ref[f, j] = value

    chunks = sems.shape[0]
    size = cells // chunks
    carry = tuple((e[2], e[3]) for e in entry)
    copies = []
    for c in reversed(range(chunks)):
        carry = upper_sweep(coef_ref, cells, z_ref, carry, store, c * size, size)
        copies.append(
            pltpu.make_async_copy(
                held_ref.at[:, pl.ds(c * size, size)], out_ref.at[:, pl.ds(c * size, size)], sems.at[c]
            )
        )
        copies[-1].start()
    for copy in copies:
        copy.wait()


def weight(a, b):
    return jnp.sqrt(1.0 - (a + b) * (a + b))


def own_table_kernel(coef_ref, vec_ref, dis_ref, tab_ref, reply_ref, mix_ref):
    _, cells, fields, width = tab_ref.shape
    total = coef_ref.shape[2]
    start = lax.axis_index("azim") * cells
    a, b, c, e = (pltpu.roll(coef_ref[kind], (total - start) % total, 1)[:, :width] for kind in range(4))
    for kind, table in enumerate((a, b, weight(a, b), c, e, weight(c, e))):
        for j in range(cells):
            tab_ref[kind, j] = over_lanes(table[:, j : j + 1], width)
    lane = lanes_of((fields, width))
    one = two = jnp.zeros((fields, width), f32)
    held = []
    for j in range(cells):
        z = jnp.where(lane == j, tab_ref[2, j], 0.0) + tab_ref[0, j] * one + tab_ref[1, j] * two
        held.append(z)
        one, two = z, one
    reply_ref[0], reply_ref[1] = one, two
    one = two = jnp.zeros((fields, width), f32)
    for j in reversed(range(cells)):
        v = tab_ref[5, j] * held[j] + tab_ref[3, j] * one + tab_ref[4, j] * two
        one, two = v, one
    reply_ref[2], reply_ref[3] = one, two
    for f in range(fields):
        mix_ref[f] = over_lanes(vec_ref[:, f : f + 1], width)
    square = (fields, fields)
    diagonal = lanes_of(square) == lax.broadcasted_iota(jnp.int32, square, 0)
    dis = jnp.sum(jnp.where(diagonal, dis_ref[...].reshape(1, fields), 0.0), axis=1, keepdims=True)
    mix_ref[fields] = over_lanes(dis, width)
    mix_ref[fields + 1] = over_lanes(1.0 - 2.0 * dis, width)


def azim_table(coef_ref, enter_ref, lone_ref):
    _, blocks, cells, width = coef_ref.shape
    fields = enter_ref.shape[0]
    own = lax.axis_index("azim")
    unit = lax.broadcasted_iota(jnp.int32, (blocks, 8, fields), 1)

    def ones(k):
        return (unit == k).astype(f32)

    one, two = ones(0), ones(1)
    held = []
    for j in range(cells):
        z = coef_ref[0, :, j : j + 1, :fields] * one + coef_ref[1, :, j : j + 1, :fields] * two
        held.append(z)
        one, two = z, one
    lower = (one, two)
    one, two = ones(2), ones(3)
    for j in reversed(range(cells)):
        c, e = coef_ref[2, :, j : j + 1, :fields], coef_ref[3, :, j : j + 1, :fields]
        v = weight(c, e) * held[j] + c * one + e * two
        one, two = v, one
    upper = (one, two)

    def entry(pair, p, m, k):
        return pair[m][p, k : k + 1]

    count = 4 * blocks
    height = -(-(count + 2) // 8) * 8
    row = lax.broadcasted_iota(jnp.int32, (height, fields), 0)

    def slot(p, k):
        return (row == 4 * (p ^ own) + k).astype(f32)

    def through(order, pair, first, source, start):
        state, entering = start, {}
        for p in order:
            entering[p] = state
            state = tuple(
                source(p, m) + entry(pair, p, m, first) * state[0] + entry(pair, p, m, first + 1) * state[1]
                for m in range(2)
            )
        return state, entering

    def closed(order, pair, first, source):
        start = tuple((row == count + k).astype(f32) for k in range(2))
        (total_one, total_two), _ = through(order, pair, first, source, start)
        a = 1.0 - total_one[count : count + 1]
        b = total_one[count + 1 : count + 2]
        c = total_two[count : count + 1]
        d = 1.0 - total_two[count + 1 : count + 2]
        scale = 1.0 / (a * d - b * c)
        live = row < count
        total_one, total_two = jnp.where(live, total_one, 0.0), jnp.where(live, total_two, 0.0)
        start = ((d * total_one + b * total_two) * scale, (c * total_one + a * total_two) * scale)
        return through(order, pair, first, source, start)[1]

    lower_in = closed(range(blocks), lower, 0, slot)

    def upper_source(p, m):
        z_one, z_two = lower_in[p]
        return slot(p, 2 + m) + entry(upper, p, m, 0) * z_one + entry(upper, p, m, 1) * z_two

    upper_in = closed(list(reversed(range(blocks))), upper, 2, upper_source)
    for i, step in enumerate(targets_of(blocks)):
        for m in range(4):
            picked = jnp.zeros((height, fields), f32)
            for p in range(blocks):
                value = lower_in[p][m] if m < 2 else upper_in[p][m - 2]
                picked = jnp.where(own == (p ^ step), value, picked)
            for f in range(fields):
                value = over_lanes(picked[:count, f : f + 1], width)
                enter_ref[f, i, m] = value
                if i == 0:
                    for again in range(2):
                        lone_ref[pl.ds(f * count * 8 + 4 * again + m, count, stride=8)] = value


def rad_table_kernel(coef_ref, own_ref, enter_ref, work_ref):
    _, rows, blocks, fields = coef_ref.shape
    width = enter_ref.shape[-1]
    own = lax.axis_index("rad")
    lower, upper = coef_ref[0], coef_ref[1]
    scale = jnp.sqrt(jnp.sqrt(1.0 + lower + upper))
    one = jnp.ones((blocks, fields), f32)
    forward, inverse, backward, outer, sums = [], [], [], [], []
    for i in range(rows):
        if i == 0:
            factor = lower[0]
            reach, total = factor, one
        else:
            factor = lower[i] * inverse[-1]
            reach, total = factor * reach, 1.0 + factor * total
        forward.append(factor)
        inverse.append(1.0 / (upper[i] + reach + total))
        backward.append(upper[i] * inverse[-1])
        outer.append(inverse[-1] * reach)
        sums.append(inverse[-1] * total)
    to_last, to_first = [None] * rows, [None] * rows
    last = inverse[-1]
    for i in reversed(range(rows)):
        to_last[i] = scale[i] * last
        last = last * forward[i]
    gain = one
    gathered = []
    for i in range(rows):
        gathered.append(gain * inverse[i])
        gain = gain * backward[i]
    first = jnp.zeros((blocks, fields), f32)
    for i in reversed(range(rows)):
        first = gathered[i] + (forward[i + 1] * first if i + 1 < rows else 0.0)
        to_first[i] = scale[i] * first
    last_before, last_after, last_sum = outer[-1], backward[-1], sums[-1]
    first_before = first_sum = 0.0
    for i in reversed(range(rows)):
        first_before = outer[i] + backward[i] * first_before
        first_sum = sums[i] + backward[i] * first_sum
    first_after = gain

    tables = ([scale[i] for i in range(rows)], forward, inverse, backward, to_last, to_first)
    step = work_ref.shape[0] // (6 * rows)
    for kind, table in enumerate(tables):
        for i in range(rows):
            work_ref[pl.ds((kind * rows + i) * step, blocks)] = table[i]
    for kind in range(6):
        picked = work_ref[pl.ds(kind * rows * step + own, rows, stride=step)]
        for f in range(fields):
            own_ref[f, kind] = over_lanes(picked[:, f : f + 1], width)

    count = 2 * blocks
    height = -(-count // 8) * 8
    row = lax.broadcasted_iota(jnp.int32, (height, fields), 0)

    def slot(p, k):
        return (row == 2 * (p ^ own) + k).astype(f32)

    def of(table, p):
        return table[p : p + 1]

    known, share, spare = {}, {}, {}
    known[0], share[0] = slot(0, 0), of(last_after, 0)
    spare[0] = of(last_sum, 0) + of(last_before, 0)
    pivots, ready = {}, {}
    for p in range(1, blocks):
        before, after, total = of(first_before, p), of(first_after, p), of(first_sum, p)
        pivots[p] = 1.0 / (after + total + before * spare[p - 1])
        ready[p] = (slot(p, 1) + before * known[p - 1]) * pivots[p]
        known[p] = slot(p, 0) + of(last_before, p) * (known[p - 1] + share[p - 1] * ready[p])
        share[p] = of(last_after, p) + of(last_before, p) * share[p - 1] * after * pivots[p]
        spare[p] = of(last_sum, p) + of(last_before, p) * pivots[p] * (
            (after + before) * spare[p - 1] + total
        )
    zero = jnp.zeros((height, fields), f32)
    above, below = {blocks - 1: zero}, {0: zero}
    for p in reversed(range(1, blocks)):
        value = ready[p] + of(first_after, p) * pivots[p] * above[p]
        above[p - 1] = value
        below[p] = known[p - 1] + share[p - 1] * value
    for i, step in enumerate(targets_of(blocks)):
        for m, entering in enumerate((below, above)):
            picked = zero
            for p in range(blocks):
                picked = jnp.where(own == (p ^ step), entering[p], picked)
            for f in range(fields):
                enter_ref[f, i, m] = over_lanes(picked[:count, f : f + 1], width)


def from_partner(values, axis, step):
    if step == 0:
        return values
    return lax.ppermute(values, axis, [(i, i ^ step) for i in range(lax.axis_size(axis))])


def local(residual, left_vec, dissip, azim_coef, radial_coef):
    fields, cells, rows, width = residual.shape
    azim_count, rad_count = lax.axis_size("azim"), lax.axis_size("rad")
    whole, flat = (fields, cells, rows, width), (fields * cells * rows, width)
    edge = call(edge_kernel, [(fields, rows, width)], residual)[0]
    halo = from_partner(edge, "axial", 1)

    own_azim, reply, mixing = call(
        own_table_kernel,
        [(6, cells, fields, width), (4, fields, width), (fields + 2, fields, width)],
        azim_coef,
        left_vec,
        dissip,
    )
    rad_blocks = radial_coef.reshape(2, fields, rad_count, rows).transpose(0, 3, 2, 1)
    own_rad, rad_enter = call(
        rad_table_kernel,
        [(fields, 6, rows, width), (fields, len(targets_of(rad_count)), 2, 2 * rad_count, width)],
        rad_blocks,
        scratch=[((6 * rows + 1) * -(-rad_count // 8) * 8, fields)],
    )

    src, states = call(
        first_kernel, [whole, (fields, 4, rows, width)], own_azim, mixing, residual, scratch=[whole]
    )
    src = src.reshape(flat)
    tables = [
        (fields, len(targets_of(azim_count)), 4, 4 * azim_count, width),
        (fields * 4 * azim_count * 8, width),
        (fields, 2, cells, width),
    ]
    turning = [(width, azim_count * cells), (4, azim_count, cells, width)]
    known = call(early_kernel, tables, azim_coef, own_rad, src, scratch=turning)
    half, small = (fields, 4, rows // 2, width), (fields, 8, width)
    message = (fields, 5, rows // 2, width)
    one, two, part, end = call(
        patch_kernel,
        [message, message, (fields, rows, width), small],
        mixing,
        own_rad,
        halo,
        states,
        reply,
        known[2],
        scratch=[(fields * 4 * rows, width)],
    )
    near, far = low_high(azim_count)
    ones = [from_partner(one, "azim", s) for s in near]
    twos = [from_partner(two, "azim", s) for s in far]
    steps = near + far[1:] + [s for s in range(azim_count) if s not in near + far]
    lone = [from_partner(end, "azim", s) for s in steps[len(near + far) - 1 :]]
    lone = [call(pass_kernel, [small], value, cost=6 * 10**8)[0] for value in lone]
    azim_enter, lone_enter, ends = call(
        late_kernel, tables, azim_coef, own_rad, src, *known, scratch=turning, aliases={3: 0, 4: 1, 5: 2}
    )
    lone_enter = lone_enter.reshape(fields, 4 * azim_count, 8, width)
    low, high = low_high(rad_count)
    ends = call(
        halo_ends_kernel, [(fields, 2, cells // 2, width)] * 2, own_rad, part, ends, scratch=[(width, width)]
    )
    ends = call(
        lambda *refs: spread_kernel(rad_count, 2, low, high, *refs),
        [(fields, 2, cells, width)] * len(high),
        rad_enter,
        *(from_partner(value, "rad", s) for s in low for value in ends),
    )
    ends = [from_partner(value, "rad", s) for s, value in zip(high, ends)]

    sums = call(
        lambda *refs: send_kernel(azim_count, near, far, *refs),
        [half] * (len(near) + len(far)),
        azim_enter,
        *ones,
        *twos,
        cost=10**11,
    )
    parts = [from_partner(value, "azim", s) for s, value in zip(far + near, sums)]
    end = call(
        lambda enter_ref, _, *refs: entry_end_kernel(steps, enter_ref, *refs),
        [small],
        lone_enter,
        sums[0],
        *ones,
        *twos[1:],
        *lone,
    )[0]
    entry_ends = [from_partner(end, "rad", s) for s in range(rad_count)]

    src = call(radial_kernel, [flat], own_rad, *ends, src, part, scratch=[flat])[0]

    chunks = 4
    return pl.pallas_call(
        lambda *refs: last_kernel(len(far), len(near), *refs),
        out_shape=jax.ShapeDtypeStruct(whole, f32),
        in_specs=[VMEM] * (len(parts + entry_ends) + 4),
        out_specs=pl.BlockSpec(memory_space=pl.ANY),
        scratch_shapes=[
            pltpu.VMEM(whole, f32),
            pltpu.VMEM((fields * 4 * rows, width), f32),
            pltpu.VMEM(whole, f32),
            pltpu.SemaphoreType.DMA((chunks,)),
        ],
        compiler_params=params,
    )(own_azim, rad_enter, own_rad, *parts, *entry_ends, src.reshape(whole))


def solution(mesh):
    placed = (P(None, "azim", "rad", "axial"), P(), P(), P(), P())
    return jax.shard_map(
        local,
        mesh=mesh,
        in_specs=placed,
        out_specs=P(None, "azim", "rad", "axial"),
        check_vma=False,
    )
```

```python
import jax
import jax.numpy as jnp
from jax import lax
from jax.experimental import pallas as pl
from jax.experimental.pallas import tpu as pltpu
from jax.sharding import PartitionSpec as P

f32 = jnp.float32
VMEM = pl.BlockSpec(memory_space=pltpu.VMEM)
params = pltpu.CompilerParams(vmem_limit_bytes=32 * 1024 * 1024)


def call(body, outs, *operands, scratch=(), cost=0, aliases={}):
    return pl.pallas_call(
        body,
        out_shape=[jax.ShapeDtypeStruct(shape, f32) for shape in outs],
        in_specs=[VMEM] * len(operands),
        out_specs=[VMEM] * len(outs),
        scratch_shapes=[pltpu.VMEM(shape, f32) for shape in scratch],
        compiler_params=params,
        input_output_aliases=aliases,
        cost_estimate=pl.CostEstimate(flops=cost, bytes_accessed=0, transcendentals=0),
    )(*operands)


def over_lanes(column, width):
    return jnp.broadcast_to(column, (column.shape[0], width))


def lanes_of(shape):
    return lax.broadcasted_iota(jnp.int32, shape, len(shape) - 1)


def low_high(count):
    split = 1 << ((count.bit_length() - 1) // 2)
    return list(range(split)), list(range(0, count, split))


def targets_of(count):
    low, high = low_high(count)
    return low + high[1:]


def far_lane(width):
    return jnp.where(lax.axis_index("axial") == 0, width - 1, 0)


def edge_kernel(res_ref, edge_ref):
    fields, cells, rows, width = res_ref.shape
    source = far_lane(width)
    lane = lanes_of((rows, width))
    packed = [jnp.zeros((rows, width), f32)] * fields
    for j in range(cells):
        for f in range(fields):
            moved = pltpu.roll(res_ref[f, j], (j - source + width) % width, 1)
            packed[f] = jnp.where(lane == j, moved, packed[f])
    for f in range(fields):
        edge_ref[f] = packed[f]


def lower_sweep(coef_ref, cells, load, z_ref, start):
    fields = len(start)

    def step(j, carry):
        source = load(j)
        out = []
        for f in range(fields):
            one, two = carry[f]
            a, b, w = (coef_ref[kind, j, f : f + 1] for kind in range(3))
            z = w * source[f] + b * two + a * one
            z_ref[f, j] = z
            out.append((z, one))
        return tuple(out)

    return lax.fori_loop(0, cells, step, start, unroll=cells)


def upper_sweep(coef_ref, cells, z_ref, start, store=None, first=0, count=None):
    fields = len(start)
    count = cells if count is None else count

    def step(i, carry):
        j = first + count - 1 - i
        out = []
        for f in range(fields):
            one, two = carry[f]
            c, e, w = (coef_ref[kind, j, f : f + 1] for kind in range(3, 6))
            v = w * z_ref[f, j] + e * two + c * one
            if store is not None:
                store(f, j, v)
            out.append((v, one))
        return tuple(out)

    return lax.fori_loop(0, count, step, start, unroll=8)


def radial_sweeps(rad_ref, f, load, ahead, back, store):
    rows = rad_ref.shape[2]

    def coef(kind, i):
        return rad_ref[f, kind, i : i + 1]

    held = []
    for i in range(rows):
        ahead = coef(0, i) * load(i) + coef(1, i) * ahead
        held.append(ahead)
    for i in reversed(range(rows)):
        back = coef(2, i) * held[i] + coef(3, i) * back
        store(i, back)


def radial_ends(rad_ref, f, load):
    last = first = None
    for i in range(rad_ref.shape[2]):
        line = load(i)
        to_last = rad_ref[f, 4, i : i + 1] * line
        to_first = rad_ref[f, 5, i : i + 1] * line
        last = to_last if last is None else last + to_last
        first = to_first if first is None else first + to_first
    return last, first


def mix(mix_ref, values):
    fields = len(values)
    return [sum(mix_ref[f, g : g + 1] * values[f] for f in range(fields)) for g in range(fields)]


def first_kernel(coef_ref, mix_ref, res_ref, src_ref, state_ref, z_ref):
    fields, cells, rows, width = res_ref.shape
    lane = lanes_of((rows, width))

    def load(j):
        out = []
        for f, c in enumerate(mix(mix_ref, [res_ref[f, j] for f in range(fields)])):
            beside = jnp.where(lane == 0, 0.0, pltpu.roll(c, 1, 1)) + jnp.where(
                lane == width - 1, 0.0, pltpu.roll(c, width - 1, 1)
            )
            src = mix_ref[fields + 1, f : f + 1] * c + mix_ref[fields, f : f + 1] * beside
            src_ref[f, j] = src
            out.append(src)
        return out

    state_ref[...] = jnp.zeros(state_ref.shape, f32)
    start = tuple((state_ref[f, 0], state_ref[f, 1]) for f in range(fields))
    carry = lower_sweep(coef_ref, cells, load, z_ref, start)
    for f in range(fields):
        state_ref[f, 0], state_ref[f, 1] = carry[f]
    start = tuple((state_ref[f, 2], state_ref[f, 3]) for f in range(fields))
    carry = upper_sweep(coef_ref, cells, z_ref, start)
    for f in range(fields):
        state_ref[f, 2], state_ref[f, 3] = carry[f]


def patch_kernel(
    mix_ref, rad_ref, halo_ref, state_ref, reply_ref, _, first_ref, second_ref, part_ref, end_ref, work_ref
):
    fields, _, rows, width = state_ref.shape
    lane = lanes_of((rows, width))
    target = far_lane(width)
    for f, h in enumerate(mix(mix_ref, [halo_ref[f] for f in range(fields)])):
        h = mix_ref[fields, f : f + 1] * h
        part_ref[f] = h
        for m in range(4):
            extra = jnp.sum(h * reply_ref[m, f : f + 1], axis=1, keepdims=True)
            tile = state_ref[f, m] + jnp.where(lane == target, extra, 0.0)
            first_ref[f, m] = tile[: rows // 2]
            second_ref[f, m] = tile[rows // 2 :]
            work_ref[pl.ds((f * 4 + m) * rows, rows)] = tile
    for f in range(fields):
        ends = radial_ends(rad_ref, f, lambda i: work_ref[pl.ds(f * 4 * rows + i, 4, stride=rows)])
        for k in range(2):
            side = slice(4 * k, 4 * k + 4)
            first_ref[f, 4, side] = second_ref[f, 4, side] = end_ref[f, side] = ends[k]


def source_ends(rad_ref, src_ref, end_ref):
    fields, _, cells, _ = end_ref.shape
    rows = rad_ref.shape[2]
    for f in range(fields):
        end_ref[f, 0], end_ref[f, 1] = radial_ends(
            rad_ref, f, lambda i: src_ref[pl.ds(f * cells * rows + i, cells, stride=rows)]
        )


def halo_ends_kernel(rad_ref, part_ref, known_ref, *refs):
    outs, turn_ref = refs[:-1], refs[-1]
    fields, _, cells, width = known_ref.shape
    lane = lanes_of((cells, width))
    target = far_lane(width)
    size = cells // len(outs)
    turn_ref[...] = jnp.zeros(turn_ref.shape, f32)
    for f in range(fields):
        ends = radial_ends(rad_ref, f, lambda i: part_ref[f, i : i + 1])
        turn_ref[2 * f : 2 * f + 1], turn_ref[2 * f + 1 : 2 * f + 2] = ends
    turned = jnp.transpose(turn_ref[...])[:cells]
    for f in range(fields):
        for k in range(2):
            moved = pltpu.roll(turned, (target - (2 * f + k) + width) % width, 1)
            value = known_ref[f, k] + jnp.where(lane == target, moved, 0.0)
            for i, out_ref in enumerate(outs):
                out_ref[f, k] = value[i * size : (i + 1) * size]


def first_half():
    return lax.axis_index("azim") < lax.axis_size("azim") // 4


def azim_blocks(coef_ref, turn_ref, block_ref):
    kinds, blocks, cells, width = block_ref.shape
    fields = coef_ref.shape[1]
    turn_ref[...] = jnp.zeros(turn_ref.shape, f32)
    for kind in range(kinds):
        turn_ref[8 * kind : 8 * kind + fields] = coef_ref[kind]
    turned = jnp.transpose(turn_ref[...])
    for kind in range(kinds):
        block_ref[kind] = pltpu.roll(turned, (width - 8 * kind) % width, 1).reshape(blocks, cells, width)


def early_kernel(coef_ref, rad_ref, src_ref, enter_ref, lone_ref, end_ref, turn_ref, block_ref):
    @pl.when(first_half())
    def _():
        azim_blocks(coef_ref, turn_ref, block_ref)
        azim_table(block_ref, enter_ref, lone_ref)
        source_ends(rad_ref, src_ref, end_ref)


def late_kernel(coef_ref, rad_ref, src_ref, _, __, ___, enter_ref, lone_ref, end_ref, turn_ref, block_ref):
    @pl.when(jnp.logical_not(first_half()))
    def _():
        azim_blocks(coef_ref, turn_ref, block_ref)
        azim_table(block_ref, enter_ref, lone_ref)
        source_ends(rad_ref, src_ref, end_ref)


def weighted(enter_ref, f, target, m, pieces):
    total = None
    for column, value in pieces:
        term = enter_ref[f, target, m, column : column + 1] * value
        total = term if total is None else total + term
    return total


def spread_kernel(count, size, near, far, enter_ref, *refs):
    arrays, sums = refs[: -len(far)], refs[-len(far) :]
    parts = len(arrays) // len(near)
    extent = arrays[0].shape[2]
    for s, out_ref in zip(far, sums):
        target = targets_of(count).index(s)
        for part in range(parts):
            for f in range(out_ref.shape[0]):
                pieces = [
                    (size * n + k, ref[f, k]) for n, ref in zip(near, arrays[part::parts]) for k in range(size)
                ]
                for m in range(size):
                    value = weighted(enter_ref, f, target, m, pieces)
                    out_ref[f, m, part * extent : (part + 1) * extent] = value


def send_kernel(count, near, far, enter_ref, *refs):
    firsts, refs = refs[: len(near)], refs[len(near) :]
    seconds, refs = refs[: len(far)], refs[len(far) :]
    spread_kernel(count, 4, near, far, enter_ref, *firsts, *refs[: len(far)])
    spread_kernel(count, 4, far, near, enter_ref, *seconds, *refs[len(far) :])


def pass_kernel(in_ref, out_ref):
    out_ref[...] = in_ref[...]


def entry_end_kernel(steps, enter_ref, *refs):
    parts, out_ref = refs[:-1], refs[-1]
    fields, _, width = out_ref.shape
    upper_rows = lax.broadcasted_iota(jnp.int32, (8, width), 0) < 4
    for f in range(fields):
        total = None
        for s, ref in zip(steps, parts):
            for k in range(4):
                here = ref.at[f, 4] if len(ref.shape) == 4 else ref.at[f]
                value = jnp.where(upper_rows, here[k : k + 1], here[4 + k : 5 + k])
                term = enter_ref[f, 4 * s + k] * value
                total = term if total is None else total + term
        out_ref[f] = total


def radial_kernel(rad_ref, *refs):
    ends, (src_ref, part_ref, out_ref, all_ref) = refs[:-4], refs[-4:]
    fields, rows, width = part_ref.shape
    cells = src_ref.shape[0] // (fields * rows)
    lane = lanes_of((rows, width))
    target = far_lane(width)
    for f in range(fields):
        for j in range(cells):
            at = pl.ds((f * cells + j) * rows, rows)
            moved = pltpu.roll(part_ref[f], (target - j + width) % width, 1)
            all_ref[at] = src_ref[at] + jnp.where(lane == target, moved, 0.0)
    for f in range(fields):
        for first in range(0, cells, 16):

            def at(i):
                return pl.ds((f * cells + first) * rows + i, 16, stride=rows)

            def store(i, value):
                out_ref[at(i)] = value

            ahead, back = (sum(ref[f, m, first : first + 16] for ref in ends) for m in range(2))
            radial_sweeps(rad_ref, f, lambda i: all_ref[at(i)], ahead, back, store)


def last_kernel(firsts, seconds, coef_ref, rad_enter_ref, rad_ref, *refs):
    parts, (src_ref, out_ref, z_ref, work_ref, held_ref, sems) = refs[:-6], refs[-6:]
    fields, cells, rows, width = src_ref.shape
    half = rows // 2
    ends = parts[firsts + seconds :]
    entry = []
    for f in range(fields):
        for m in range(4):
            base = (f * 4 + m) * rows
            work_ref[pl.ds(base, half)] = sum(ref[f, m] for ref in parts[:firsts])
            work_ref[pl.ds(base + half, half)] = sum(ref[f, m] for ref in parts[firsts : firsts + seconds])
        pieces = [(2 * s + k, ref[f, 4 * k : 4 * k + 4]) for s, ref in enumerate(ends) for k in range(2)]

        def store(i, value):
            work_ref[pl.ds(f * 4 * rows + i, 4, stride=rows)] = value

        radial_sweeps(
            rad_ref,
            f,
            lambda i: work_ref[pl.ds(f * 4 * rows + i, 4, stride=rows)],
            *(weighted(rad_enter_ref, f, 0, m, pieces) for m in range(2)),
            store,
        )
        entry.append([work_ref[pl.ds((f * 4 + m) * rows, rows)] for m in range(4)])
    lower_sweep(
        coef_ref,
        cells,
        lambda j: [src_ref[f, j] for f in range(fields)],
        z_ref,
        tuple((e[0], e[1]) for e in entry),
    )

    def store(f, j, value):
        held_ref[f, j] = value

    chunks = sems.shape[0]
    size = cells // chunks
    carry = tuple((e[2], e[3]) for e in entry)
    copies = []
    for c in reversed(range(chunks)):
        carry = upper_sweep(coef_ref, cells, z_ref, carry, store, c * size, size)
        copies.append(
            pltpu.make_async_copy(
                held_ref.at[:, pl.ds(c * size, size)], out_ref.at[:, pl.ds(c * size, size)], sems.at[c]
            )
        )
        copies[-1].start()
    for copy in copies:
        copy.wait()


def weight(a, b):
    return jnp.sqrt(1.0 - (a + b) * (a + b))


def own_table_kernel(coef_ref, vec_ref, dis_ref, tab_ref, reply_ref, mix_ref):
    _, cells, fields, width = tab_ref.shape
    total = coef_ref.shape[2]
    start = lax.axis_index("azim") * cells
    a, b, c, e = (pltpu.roll(coef_ref[kind], (total - start) % total, 1)[:, :width] for kind in range(4))
    for kind, table in enumerate((a, b, weight(a, b), c, e, weight(c, e))):
        for j in range(cells):
            tab_ref[kind, j] = over_lanes(table[:, j : j + 1], width)
    lane = lanes_of((fields, width))
    one = two = jnp.zeros((fields, width), f32)
    held = []
    for j in range(cells):
        z = jnp.where(lane == j, tab_ref[2, j], 0.0) + tab_ref[0, j] * one + tab_ref[1, j] * two
        held.append(z)
        one, two = z, one
    reply_ref[0], reply_ref[1] = one, two
    one = two = jnp.zeros((fields, width), f32)
    for j in reversed(range(cells)):
        v = tab_ref[5, j] * held[j] + tab_ref[3, j] * one + tab_ref[4, j] * two
        one, two = v, one
    reply_ref[2], reply_ref[3] = one, two
    for f in range(fields):
        mix_ref[f] = over_lanes(vec_ref[:, f : f + 1], width)
    square = (fields, fields)
    diagonal = lanes_of(square) == lax.broadcasted_iota(jnp.int32, square, 0)
    dis = jnp.sum(jnp.where(diagonal, dis_ref[...].reshape(1, fields), 0.0), axis=1, keepdims=True)
    mix_ref[fields] = over_lanes(dis, width)
    mix_ref[fields + 1] = over_lanes(1.0 - 2.0 * dis, width)


def azim_table(coef_ref, enter_ref, lone_ref):
    _, blocks, cells, width = coef_ref.shape
    fields = enter_ref.shape[0]
    own = lax.axis_index("azim")
    unit = lax.broadcasted_iota(jnp.int32, (blocks, 8, fields), 1)

    def ones(k):
        return (unit == k).astype(f32)

    one, two = ones(0), ones(1)
    held = []
    for j in range(cells):
        z = coef_ref[0, :, j : j + 1, :fields] * one + coef_ref[1, :, j : j + 1, :fields] * two
        held.append(z)
        one, two = z, one
    lower = (one, two)
    one, two = ones(2), ones(3)
    for j in reversed(range(cells)):
        c, e = coef_ref[2, :, j : j + 1, :fields], coef_ref[3, :, j : j + 1, :fields]
        v = weight(c, e) * held[j] + c * one + e * two
        one, two = v, one
    upper = (one, two)

    def entry(pair, p, m, k):
        return pair[m][p, k : k + 1]

    count = 4 * blocks
    height = -(-(count + 2) // 8) * 8
    row = lax.broadcasted_iota(jnp.int32, (height, fields), 0)

    def slot(p, k):
        return (row == 4 * (p ^ own) + k).astype(f32)

    def through(order, pair, first, source, start):
        state, entering = start, {}
        for p in order:
            entering[p] = state
            state = tuple(
                source(p, m) + entry(pair, p, m, first) * state[0] + entry(pair, p, m, first + 1) * state[1]
                for m in range(2)
            )
        return state, entering

    def closed(order, pair, first, source):
        start = tuple((row == count + k).astype(f32) for k in range(2))
        (total_one, total_two), _ = through(order, pair, first, source, start)
        a = 1.0 - total_one[count : count + 1]
        b = total_one[count + 1 : count + 2]
        c = total_two[count : count + 1]
        d = 1.0 - total_two[count + 1 : count + 2]
        scale = 1.0 / (a * d - b * c)
        live = row < count
        total_one, total_two = jnp.where(live, total_one, 0.0), jnp.where(live, total_two, 0.0)
        start = ((d * total_one + b * total_two) * scale, (c * total_one + a * total_two) * scale)
        return through(order, pair, first, source, start)[1]

    lower_in = closed(range(blocks), lower, 0, slot)

    def upper_source(p, m):
        z_one, z_two = lower_in[p]
        return slot(p, 2 + m) + entry(upper, p, m, 0) * z_one + entry(upper, p, m, 1) * z_two

    upper_in = closed(list(reversed(range(blocks))), upper, 2, upper_source)
    for i, step in enumerate(targets_of(blocks)):
        for m in range(4):
            picked = jnp.zeros((height, fields), f32)
            for p in range(blocks):
                value = lower_in[p][m] if m < 2 else upper_in[p][m - 2]
                picked = jnp.where(own == (p ^ step), value, picked)
            for f in range(fields):
                value = over_lanes(picked[:count, f : f + 1], width)
                enter_ref[f, i, m] = value
                if i == 0:
                    for again in range(2):
                        lone_ref[pl.ds(f * count * 8 + 4 * again + m, count, stride=8)] = value


def rad_table_kernel(coef_ref, own_ref, enter_ref, work_ref):
    _, rows, blocks, fields = coef_ref.shape
    width = enter_ref.shape[-1]
    own = lax.axis_index("rad")
    lower, upper = coef_ref[0], coef_ref[1]
    scale = jnp.sqrt(jnp.sqrt(1.0 + lower + upper))
    one = jnp.ones((blocks, fields), f32)
    forward, inverse, backward, outer, sums = [], [], [], [], []
    for i in range(rows):
        if i == 0:
            factor = lower[0]
            reach, total = factor, one
        else:
            factor = lower[i] * inverse[-1]
            reach, total = factor * reach, 1.0 + factor * total
        forward.append(factor)
        inverse.append(1.0 / (upper[i] + reach + total))
        backward.append(upper[i] * inverse[-1])
        outer.append(inverse[-1] * reach)
        sums.append(inverse[-1] * total)
    to_last, to_first = [None] * rows, [None] * rows
    last = inverse[-1]
    for i in reversed(range(rows)):
        to_last[i] = scale[i] * last
        last = last * forward[i]
    gain = one
    gathered = []
    for i in range(rows):
        gathered.append(gain * inverse[i])
        gain = gain * backward[i]
    first = jnp.zeros((blocks, fields), f32)
    for i in reversed(range(rows)):
        first = gathered[i] + (forward[i + 1] * first if i + 1 < rows else 0.0)
        to_first[i] = scale[i] * first
    last_before, last_after, last_sum = outer[-1], backward[-1], sums[-1]
    first_before = first_sum = 0.0
    for i in reversed(range(rows)):
        first_before = outer[i] + backward[i] * first_before
        first_sum = sums[i] + backward[i] * first_sum
    first_after = gain

    tables = ([scale[i] for i in range(rows)], forward, inverse, backward, to_last, to_first)
    step = work_ref.shape[0] // (6 * rows)
    for kind, table in enumerate(tables):
        for i in range(rows):
            work_ref[pl.ds((kind * rows + i) * step, blocks)] = table[i]
    for kind in range(6):
        picked = work_ref[pl.ds(kind * rows * step + own, rows, stride=step)]
        for f in range(fields):
            own_ref[f, kind] = over_lanes(picked[:, f : f + 1], width)

    count = 2 * blocks
    height = -(-count // 8) * 8
    row = lax.broadcasted_iota(jnp.int32, (height, fields), 0)

    def slot(p, k):
        return (row == 2 * (p ^ own) + k).astype(f32)

    def of(table, p):
        return table[p : p + 1]

    known, share, spare = {}, {}, {}
    known[0], share[0] = slot(0, 0), of(last_after, 0)
    spare[0] = of(last_sum, 0) + of(last_before, 0)
    pivots, ready = {}, {}
    for p in range(1, blocks):
        before, after, total = of(first_before, p), of(first_after, p), of(first_sum, p)
        pivots[p] = 1.0 / (after + total + before * spare[p - 1])
        ready[p] = (slot(p, 1) + before * known[p - 1]) * pivots[p]
        known[p] = slot(p, 0) + of(last_before, p) * (known[p - 1] + share[p - 1] * ready[p])
        share[p] = of(last_after, p) + of(last_before, p) * share[p - 1] * after * pivots[p]
        spare[p] = of(last_sum, p) + of(last_before, p) * pivots[p] * (
            (after + before) * spare[p - 1] + total
        )
    zero = jnp.zeros((height, fields), f32)
    above, below = {blocks - 1: zero}, {0: zero}
    for p in reversed(range(1, blocks)):
        value = ready[p] + of(first_after, p) * pivots[p] * above[p]
        above[p - 1] = value
        below[p] = known[p - 1] + share[p - 1] * value
    for i, step in enumerate(targets_of(blocks)):
        for m, entering in enumerate((below, above)):
            picked = zero
            for p in range(blocks):
                picked = jnp.where(own == (p ^ step), entering[p], picked)
            for f in range(fields):
                enter_ref[f, i, m] = over_lanes(picked[:count, f : f + 1], width)


def from_partner(values, axis, step):
    if step == 0:
        return values
    return lax.ppermute(values, axis, [(i, i ^ step) for i in range(lax.axis_size(axis))])


def local(residual, left_vec, dissip, azim_coef, radial_coef):
    fields, cells, rows, width = residual.shape
    azim_count, rad_count = lax.axis_size("azim"), lax.axis_size("rad")
    whole, flat = (fields, cells, rows, width), (fields * cells * rows, width)
    edge = call(edge_kernel, [(fields, rows, width)], residual)[0]
    halo = from_partner(edge, "axial", 1)

    own_azim, reply, mixing = call(
        own_table_kernel,
        [(6, cells, fields, width), (4, fields, width), (fields + 2, fields, width)],
        azim_coef,
        left_vec,
        dissip,
    )
    rad_blocks = radial_coef.reshape(2, fields, rad_count, rows).transpose(0, 3, 2, 1)
    own_rad, rad_enter = call(
        rad_table_kernel,
        [(fields, 6, rows, width), (fields, len(targets_of(rad_count)), 2, 2 * rad_count, width)],
        rad_blocks,
        scratch=[((6 * rows + 1) * -(-rad_count // 8) * 8, fields)],
    )

    src, states = call(
        first_kernel, [whole, (fields, 4, rows, width)], own_azim, mixing, residual, scratch=[whole]
    )
    src = src.reshape(flat)
    tables = [
        (fields, len(targets_of(azim_count)), 4, 4 * azim_count, width),
        (fields * 4 * azim_count * 8, width),
        (fields, 2, cells, width),
    ]
    turning = [(width, azim_count * cells), (4, azim_count, cells, width)]
    known = call(early_kernel, tables, azim_coef, own_rad, src, scratch=turning)
    half, small = (fields, 4, rows // 2, width), (fields, 8, width)
    message = (fields, 5, rows // 2, width)
    one, two, part, end = call(
        patch_kernel,
        [message, message, (fields, rows, width), small],
        mixing,
        own_rad,
        halo,
        states,
        reply,
        known[2],
        scratch=[(fields * 4 * rows, width)],
    )
    near, far = low_high(azim_count)
    ones = [from_partner(one, "azim", s) for s in near]
    twos = [from_partner(two, "azim", s) for s in far]
    steps = near + far[1:] + [s for s in range(azim_count) if s not in near + far]
    lone = [from_partner(end, "azim", s) for s in steps[len(near + far) - 1 :]]
    lone = [call(pass_kernel, [small], value, cost=6 * 10**8)[0] for value in lone]
    azim_enter, lone_enter, ends = call(
        late_kernel, tables, azim_coef, own_rad, src, *known, scratch=turning, aliases={3: 0, 4: 1, 5: 2}
    )
    lone_enter = lone_enter.reshape(fields, 4 * azim_count, 8, width)
    low, high = low_high(rad_count)
    ends = call(
        halo_ends_kernel, [(fields, 2, cells // 2, width)] * 2, own_rad, part, ends, scratch=[(width, width)]
    )
    ends = call(
        lambda *refs: spread_kernel(rad_count, 2, low, high, *refs),
        [(fields, 2, cells, width)] * len(high),
        rad_enter,
        *(from_partner(value, "rad", s) for s in low for value in ends),
    )
    ends = [from_partner(value, "rad", s) for s, value in zip(high, ends)]

    sums = call(
        lambda *refs: send_kernel(azim_count, near, far, *refs),
        [half] * (len(near) + len(far)),
        azim_enter,
        *ones,
        *twos,
        cost=10**11,
    )
    parts = [from_partner(value, "azim", s) for s, value in zip(far + near, sums)]
    end = call(
        lambda enter_ref, _, *refs: entry_end_kernel(steps, enter_ref, *refs),
        [small],
        lone_enter,
        sums[0],
        *ones,
        *twos[1:],
        *lone,
    )[0]
    entry_ends = [from_partner(end, "rad", s) for s in range(rad_count)]

    src = call(radial_kernel, [flat], own_rad, *ends, src, part, scratch=[flat])[0]

    chunks = 4
    return pl.pallas_call(
        lambda *refs: last_kernel(len(far), len(near), *refs),
        out_shape=jax.ShapeDtypeStruct(whole, f32),
        in_specs=[VMEM] * (len(parts + entry_ends) + 4),
        out_specs=pl.BlockSpec(memory_space=pl.ANY),
        scratch_shapes=[
            pltpu.VMEM(whole, f32),
            pltpu.VMEM((fields * 4 * rows, width), f32),
            pltpu.VMEM(whole, f32),
            pltpu.SemaphoreType.DMA((chunks,)),
        ],
        compiler_params=params,
    )(own_azim, rad_enter, own_rad, *parts, *entry_ends, src.reshape(whole))


def solution(mesh):
    placed = (P(None, "azim", "rad", "axial"), P(), P(), P(), P())
    return jax.shard_map(
        local,
        mesh=mesh,
        in_specs=placed,
        out_specs=P(None, "azim", "rad", "axial"),
        check_vma=False,
    )
```
